32 devices in a mesh: row: 4 (over y, core), col: 8 (over z, x).
Axes of the slice: x: 2, y: 2, z: 4, core: 2. Of those that a mesh axis runs over, the one named last changes fastest.
Arguments:
- vectors: bfloat16 [24576, 1024], P(('row', 'col')), may hold values from -6 to 6
- ham_blocks: bfloat16 [192, 5, 128, 128], P(('row', 'col')), as said below
- ham_columns: int32 [192, 5], P(('row', 'col')), may hold values from 0 to 191, as said below
- bounds: float32 [2], replicated, may hold values from -1 to 2.6, as said below
Outputs:
- filtered: bfloat16 [24576, 1024], P(('row', 'col'))
The draws below stay inside these ranges and needn't reach their ends.
Inputs may be any that keep to these rules, and one draw needn't show every extreme that they name: `ham_columns`: each slot of block row g names a block column (g + o) mod 192 with -2 <= o <= 2; some slot names g itself, every other distance at most once. Slots whose offset is absent name g itself and carry zero blocks; the one slot with offset 0 carries the diagonal block. `ham_blocks`: H is symmetric: the block of block row g at block column h is the transpose of the block of block row h at block column g. bounds[0] < bounds[1].
All inputs are finite; a program needn't handle non-finite values.
Results may differ from the reference program's by a relative error of at most 0.0045.
Values may be sent and summed in bfloat16 or wider, within the bound.
No kernel may reach another device: no remote copies, remote signals or barrier semaphores. Data moves between devices by JAX's collectives and lax.ppermute only.
A program may use at most 64 MiB of HBM per device.

```python
import math
import jax
import jax.numpy as jnp
from jax import lax

BLOCK = 128
VECTORS = 1024
REACH = 2
SLOTS = 5
DEG = 2
NBLOCKS = 192
ORBITALS = 24576


def band_pattern(key):
    present_pair = jax.random.randint(jax.random.fold_in(key, 31), (NBLOCKS, REACH), 0, 5) < 3
    row_ids = jnp.arange(NBLOCKS, dtype=jnp.int32).reshape(-1, 1)
    distance = jnp.arange(1, REACH + 1, dtype=jnp.int32).reshape(1, -1)
    upward = present_pair
    downward = present_pair[jnp.remainder(row_ids - distance, NBLOCKS), distance - 1]
    present = jnp.concatenate([jnp.ones((NBLOCKS, 1), dtype=bool), upward, downward], axis=1)
    offsets = jnp.concatenate([jnp.zeros((1,), jnp.int32), jnp.arange(1, REACH + 1, dtype=jnp.int32), -jnp.arange(1, REACH + 1, dtype=jnp.int32)])
    order_keys = jax.random.split(jax.random.fold_in(key, 32), NBLOCKS)
    orders = jax.vmap(lambda item: jax.random.permutation(item, SLOTS))(order_keys).astype(jnp.int32)
    slot_offset = offsets[orders]
    slot_present = jnp.take_along_axis(present, orders, axis=1)
    columns = jnp.where(slot_present, jnp.remainder(row_ids + slot_offset, NBLOCKS), row_ids)
    return (columns.astype(jnp.int32), slot_offset, slot_present)


def draw_ham_columns(key, part):
    columns, slot_offset, slot_present = band_pattern(key)
    return columns


def draw_ham_blocks(key, part):
    columns, slot_offset, slot_present = band_pattern(key)
    row_ids = jnp.broadcast_to(jnp.arange(NBLOCKS, dtype=jnp.int32).reshape(-1, 1), columns.shape)
    value_key = jax.random.fold_in(key, 33)
    scale = float((1.0 + 1.2 * REACH) * BLOCK) ** (-0.5)

    def one_block(items):
        row_id = items[0]
        offset = items[1]
        alive = items[2]
        distance = jnp.abs(offset)
        lower = jnp.where(offset < 0, jnp.remainder(row_id + offset, NBLOCKS), row_id)
        item = jax.random.fold_in(value_key, lower * (REACH + 1) + distance)
        raw = jax.random.normal(item, (BLOCK, BLOCK), jnp.float32)
        flipped = jnp.swapaxes(raw, 0, 1)
        chosen = jnp.where(offset > 0, raw, jnp.where(offset < 0, flipped, (raw + flipped) * math.sqrt(0.5)))
        return (chosen * scale * alive.astype(jnp.float32)).astype(jnp.bfloat16)
    stacked = jnp.stack([row_ids.reshape(-1), slot_offset.reshape(-1), slot_present.reshape(-1).astype(jnp.int32)], axis=1)
    blocks = lax.map(one_block, stacked)
    return blocks.reshape(NBLOCKS, SLOTS, BLOCK, BLOCK)


def draw_bounds(key, part):
    low_key, high_key = jax.random.split(jax.random.fold_in(key, 21))
    lower = jax.random.uniform(low_key, (), jnp.float32, -1.0, -0.2)
    upper = jax.random.uniform(high_key, (), jnp.float32, 2.0, 2.6)
    return jnp.stack([lower, upper])


def level_of(own_key, extent, pieces, low, high):
    factor_of, own = 1.0, jax.random.fold_in(own_key, 6)
    for axis_at, shards_of in pieces:
        draws = jnp.exp(jax.random.uniform(jax.random.fold_in(own, axis_at), (shards_of,), jnp.float32, low / len(pieces), high / len(pieces)))
        factor_of = factor_of * jnp.repeat(draws, extent[axis_at] // shards_of).reshape([-1 if axis == axis_at else 1 for axis in range(len(extent))])
    return factor_of


def bell_draw(own_key, extent, width, most, cuts=(), held_as=jnp.bfloat16):
    gain = level_of(own_key, extent, cuts, -0.22, 0.18) if cuts else 1.0
    array = jax.random.normal(own_key, extent, jnp.float32) * width * gain
    return jnp.minimum(jnp.maximum(array, -most), most).astype(held_as)


def setup_inputs(seed: int = 0) -> dict:
    arg_keys = jax.random.split(jax.random.key(seed), 5)
    vectors = bell_draw(arg_keys[0], (ORBITALS, VECTORS), 1.0, 6.0, ((0, 32),))
    ham_blocks = draw_ham_blocks(jax.random.fold_in(arg_keys[4], 71), 0)
    ham_columns = draw_ham_columns(jax.random.fold_in(arg_keys[4], 71), 0)
    bounds = draw_bounds(jax.random.fold_in(arg_keys[4], 71), 0)
    return dict(vectors=vectors, ham_blocks=ham_blocks, ham_columns=ham_columns, bounds=bounds)


def apply_hamiltonian(current, ham_blocks, ham_columns):
    grid = current.reshape(NBLOCKS, BLOCK, VECTORS)

    def one_row(index):
        blocks = ham_blocks[index].astype(jnp.float32)
        picked = grid[ham_columns[index].astype(jnp.int32)].astype(jnp.float32)
        return jnp.einsum("kij,kjm->im", blocks, picked, precision=lax.Precision.HIGHEST)

    image = lax.map(one_row, jnp.arange(NBLOCKS, dtype=jnp.int32))
    return image.reshape(NBLOCKS * BLOCK, VECTORS)


def reference(vectors, ham_blocks, ham_columns, bounds):
    center = 0.5 * (bounds[1] + bounds[0])
    halfwidth = 0.5 * (bounds[1] - bounds[0])
    previous = vectors
    current = vectors
    for degree_step in range(DEG):
        image = apply_hamiltonian(current, ham_blocks, ham_columns)
        shifted = (image - center * current.astype(jnp.float32)) / halfwidth
        if degree_step == 0:
            updated = shifted
        else:
            updated = 2.0 * shifted - previous.astype(jnp.float32)
        previous, current = current, updated.astype(jnp.bfloat16)
    return current
```

```python
import functools

import jax
import jax.numpy as jnp
from jax import lax
from jax.experimental import pallas as pl
from jax.experimental.pallas import tpu as pltpu
from jax.sharding import PartitionSpec as P

AXES = ("row", "col")
B = 128
PAIR = 2 * B
HEAD = 6 * B
X_SLABS = (5, 3)
D_SLABS = (3, 5)
LIMIT = pltpu.CompilerParams(vmem_limit_bytes=16 * 1024 * 1024)
FREE = pl.CostEstimate(flops=0, bytes_accessed=0, transcendentals=0)


def place():
    return lax.axis_index("row") * lax.axis_size("col") + lax.axis_index("col")


def dot(a, b):
    return jnp.dot(a, b, preferred_element_type=jnp.float32)


def turn(block):
    return block.astype(jnp.float32).T.astype(block.dtype)


def natural(pair, pairs):
    odd = lax.rem(place(), 2)
    return pl.ds(pl.multiple_of(jnp.where(odd == 1, pairs - 1 - pair, pair) * PAIR, PAIR), PAIR)


def head(c):
    return HEAD if c == 0 else 0


def pack_kernel(total_blocks, cols_ref, blocks_ref, v_ref, own_ref, *sent):
    x_refs, d_refs = sent[: len(X_SLABS)], sent[len(X_SLABS) :]
    here = place()
    odd = lax.rem(here, 2)
    rows_here, slots = blocks_ref.shape[0], blocks_ref.shape[1]
    pairs = rows_here // 2
    first = here * rows_here
    own_ref[...] = jnp.zeros_like(own_ref)
    for r in range(rows_here):
        j, i = r // 2, r % 2
        row = pl.multiple_of(jnp.where(odd == 1, pairs - 1 - j, j) * PAIR + i * B, B)
        for k in range(slots):
            offset = lax.rem(cols_ref[r, k] - (first + r) + 2 + total_blocks, total_blocks)
            at = offset + i
            turned = (2 - at // 2) * 2 + lax.rem(at, 2)
            col = pl.multiple_of(jnp.where(odd == 1, turned, at) * B, B)
            own_ref[pl.ds(row, B), pl.ds(col, B)] += blocks_ref[r, k]
    last = (pairs - 1) * PAIR
    for out, row, near, mid in ((x_refs[0], last, PAIR, 0), (d_refs[0], 0, PAIR, 2 * PAIR)):
        out[0:B, :] = own_ref[row : row + B, near : near + B]
        out[B : 2 * B, :] = own_ref[row : row + B, near + B : near + 2 * B]
        out[2 * B : 3 * B, :] = own_ref[row + B : row + 2 * B, near + B : near + 2 * B]
        out[3 * B : 4 * B, :] = own_ref[row : row + B, mid : mid + B]
        out[4 * B : 5 * B, :] = (
            own_ref[row : row + B, mid + B : mid + 2 * B]
            + own_ref[row + B : row + 2 * B, mid : mid + B]
        )
        out[5 * B : 6 * B, :] = own_ref[row + B : row + 2 * B, mid + B : mid + 2 * B]
    for refs, split, edge in ((x_refs, X_SLABS, pairs - 1), (d_refs, D_SLABS, 0)):
        slab = 0
        for c, slabs in enumerate(split):
            for s in range(slabs):
                at = head(c) + s * PAIR
                refs[c][at : at + PAIR, :] = v_ref[
                    natural(edge, pairs), slice(slab * B, (slab + 1) * B)
                ]
                slab += 1


def scales(bounds_ref):
    low, high = bounds_ref[0], bounds_ref[1]
    return 0.5 * (high + low), 0.5 * (high - low)


def core_kernel(bounds_ref, v_ref, own_ref, one_ref, g0_ref, g2_ref, h0_ref, h1_ref, h2_ref):
    pairs = v_ref.shape[0] // PAIR
    center, halfwidth = scales(bounds_ref)
    for at in range(0, v_ref.shape[1], PAIR):
        lanes = slice(at, at + PAIR)
        v0, v1, v2 = (v_ref[natural(j, pairs), lanes] for j in range(3))
        v = jnp.concatenate([v0, v1, v2], axis=0)
        g0_ref[:, lanes] = dot(own_ref[0:PAIR, PAIR:], v[: 2 * PAIR])
        g2_ref[:, lanes] = dot(own_ref[2 * PAIR :, : 2 * PAIR], v[PAIR:])
        image = dot(own_ref[PAIR : 2 * PAIR, :], v)
        one = ((image - center * v1.astype(jnp.float32)) / halfwidth).astype(one_ref.dtype)
        one_ref[:, lanes] = one
        h0_ref[:, lanes] = dot(own_ref[0:PAIR, 2 * PAIR :], one)
        h1_ref[:, lanes] = dot(own_ref[PAIR : 2 * PAIR, PAIR : 2 * PAIR], one)
        h2_ref[:, lanes] = dot(own_ref[2 * PAIR :, 0:PAIR], one)


def halo_kernel(side, own_ref, sent_ref, halo_ref):
    odd = lax.rem(place(), 2)
    halo_ref[...] = jnp.zeros_like(halo_ref)
    if side == 0:
        known, low = own_ref[0:PAIR, 0:PAIR], odd
    else:
        known, low = own_ref[2 * PAIR :, 2 * PAIR :], 1 - odd
    halo_ref[:, 0:PAIR] = turn(known)
    near, far = PAIR, 2 * PAIR
    halo_ref[0:B, near : near + B] = sent_ref[0:B, :]
    halo_ref[0:B, near + B : near + PAIR] = sent_ref[B : 2 * B, :]
    halo_ref[B:PAIR, near : near + B] = turn(sent_ref[B : 2 * B, :])
    halo_ref[B:PAIR, near + B : near + PAIR] = sent_ref[2 * B : 3 * B, :]
    halo_ref[0:B, far : far + B] = sent_ref[3 * B : 4 * B, :]
    halo_ref[
        pl.ds(pl.multiple_of(low * B, B), B), pl.ds(pl.multiple_of(far + (1 - low) * B, B), B)
    ] = sent_ref[4 * B : 5 * B, :]
    halo_ref[B:PAIR, far + B : far + PAIR] = sent_ref[5 * B : 6 * B, :]


def side_kernel(
    side, first_slab, slabs, top, bounds_ref, v_ref, near_ref, low_ref, high_ref, own_ref, halo_ref,
    one_ref, g_ref, h_ref, h1_ref, *rest
):
    if side == 0:
        h1_out, out_ref, end_ref, sems = rest[-4:]
    else:
        out_ref, end_ref, mid_ref, sems = rest[-4:]
    pairs = v_ref.shape[0] // PAIR
    center, halfwidth = scales(bounds_ref)
    edge = 0 if side == 0 else 2
    rows = slice(edge * PAIR, (edge + 1) * PAIR)
    outward = slice(0, PAIR) if side == 0 else slice(2 * PAIR, 3 * PAIR)
    step = 2 if slabs % 2 == 0 else slabs
    for s in range(0, slabs, step):
        lanes = slice((first_slab + s) * B, (first_slab + s + step) * B)
        here = slice(s * B, (s + step) * B)
        near = jnp.concatenate(
            [near_ref[top + t * PAIR : top + (t + 1) * PAIR, :] for t in range(s, s + step)], axis=1
        )
        v = v_ref[natural(edge, pairs), lanes]
        stack = jnp.concatenate([v, near, low_ref[:, lanes], high_ref[:, lanes]], axis=0)
        v32 = v.astype(jnp.float32)
        image = g_ref[:, lanes] + dot(own_ref[rows, outward], near)
        edge_one = ((image - center * v32) / halfwidth).astype(v.dtype)
        image = dot(halo_ref[...], stack)
        near_one = ((image - center * near.astype(jnp.float32)) / halfwidth).astype(v.dtype)
        h1 = h1_ref[:, lanes] + dot(own_ref[PAIR : 2 * PAIR, outward], edge_one)
        if side == 0:
            h1_out[:, lanes] = h1
        else:
            one, v1 = one_ref[:, lanes].astype(jnp.float32), v_ref[natural(1, pairs), lanes].astype(jnp.float32)
            mid_ref[:, here] = (2.0 * ((h1 - center * one) / halfwidth) - v1).astype(v.dtype)
        image = h_ref[:, lanes] + (
            dot(own_ref[rows, PAIR : 2 * PAIR], edge_one) + dot(own_ref[rows, outward], near_one)
        )
        end_ref[:, here] = (
            2.0 * ((image - center * edge_one.astype(jnp.float32)) / halfwidth) - v32
        ).astype(v.dtype)
    lanes = slice(first_slab * B, (first_slab + slabs) * B)
    copies = [pltpu.make_async_copy(end_ref, out_ref.at[natural(edge, pairs), lanes], sems.at[0])]
    if side:
        copies.append(pltpu.make_async_copy(mid_ref, out_ref.at[natural(1, pairs), lanes], sems.at[1]))
    for copy in copies:
        copy.start()
    for copy in copies:
        copy.wait()


def whole(ref_space=pltpu.VMEM):
    return pl.BlockSpec(memory_space=ref_space)


def call(body, out_shape, args, name, aliases=None, scratch=()):
    aliases = aliases or {}
    outs = out_shape if isinstance(out_shape, list) else [out_shape]
    spaces = [
        pltpu.SMEM if a.size < 1024 else pl.ANY if isinstance(outs[aliases.get(i, 0)], jax.ShapeDtypeStruct) and i in aliases else pltpu.VMEM
        for i, a in enumerate(args)
    ]
    return pl.pallas_call(
        body,
        out_shape=out_shape,
        in_specs=[whole(space) for space in spaces],
        out_specs=jax.tree.map(
            lambda o: whole(pl.ANY if isinstance(o, jax.ShapeDtypeStruct) else pltpu.VMEM), out_shape
        ),
        scratch_shapes=scratch,
        input_output_aliases=aliases,
        compiler_params=LIMIT,
        cost_estimate=FREE,
        name=name,
    )(
        *(
            pltpu.with_memory_space_constraint(a, pltpu.VMEM) if space == pltpu.VMEM else a
            for a, space in zip(args, spaces, strict=True)
        )
    )


def per_device(vectors, ham_blocks, ham_columns, bounds):
    rows, vec_width = vectors.shape
    rows_here = ham_blocks.shape[0]
    ring = lax.axis_size(AXES)
    dtype = vectors.dtype
    swap_x = [(i, i ^ 1) for i in range(ring)]
    swap_d = [(i, (i + 1) % ring if i % 2 else (i - 1) % ring) for i in range(ring)]
    onward = [(i, (i - 2) % ring if i % 2 else (i + 2) % ring) for i in range(ring)]
    send = functools.partial(lax.ppermute, axis_name=AXES)

    def message(c, slabs):
        return pltpu.VMEM((head(c) + slabs * PAIR, B), dtype)

    middle = [lax.slice_in_dim(vectors, rows // 2 + at, rows // 2 + at + B, axis=0) for at in (-B, 0)]
    own, *parts = call(
        functools.partial(pack_kernel, ring * rows_here),
        [pltpu.VMEM((rows, 3 * PAIR), dtype)]
        + [message(c, slabs) for split in (X_SLABS, D_SLABS) for c, slabs in enumerate(split)],
        [ham_columns, ham_blocks, vectors],
        "pack",
    )
    to_x, to_d = parts[: len(X_SLABS)], parts[len(X_SLABS) :]
    def after(token, value):
        return lax.optimization_barrier((token, value))

    m0, m1 = (send(part, perm=swap_x) for part in middle)
    m0, to_d[0] = after(m0, to_d[0])
    m1, to_d[1] = after(m1, to_d[1])
    far_x = [m0, m1]
    far_d = [send(part, perm=onward) for part in far_x]
    got = [send(part, perm=swap_x) for part in to_d]
    far_d[0], to_x[0] = after(far_d[0], to_x[0])
    got[0], to_x[0] = after(got[0], to_x[0])
    far_d[1], got[1] = after(far_d[1], got[1])
    got[1], to_x[1] = after(got[1], to_x[1])
    near_d = [send(part, perm=onward) for part in got]
    near_x = [send(part, perm=swap_x) for part in to_x]

    wide = lambda kind: pltpu.VMEM((PAIR, vec_width), kind)
    one, g0, g2, h0, h1, h2 = call(
        core_kernel, [wide(dtype)] + [wide(jnp.float32)] * 5, [bounds, vectors, own], "core"
    )
    band = pltpu.VMEM((PAIR, 3 * PAIR), dtype)
    result, out = None, jax.ShapeDtypeStruct((rows, vec_width), dtype)
    for side, near, split, far, g, h in (
        (0, near_d, D_SLABS, far_d, g0, h0),
        (1, near_x, X_SLABS, far_x, g2, h2),
    ):
        if result is not None:
            near[0], result = lax.optimization_barrier((near[0], result))
        halo = call(functools.partial(halo_kernel, side), band, [own, near[0]], "halo")
        first_slab = 0
        for c, slabs in enumerate(split):
            args = [bounds, vectors, near[c], *far, own, halo, one, g, h, h1]
            outs, aliases = [out], {}
            if side == 0:
                outs, aliases = [wide(jnp.float32), out], {len(args) - 1: 0}
            if result is not None:
                aliases[len(args)] = len(outs) - 1
                args.append(result)
            *rest, result = call(
                functools.partial(side_kernel, side, first_slab, slabs, head(c)),
                outs,
                args,
                "side",
                aliases=aliases,
                scratch=[pltpu.VMEM((PAIR, slabs * B), dtype)] * (1 + side)
                + [pltpu.SemaphoreType.DMA((2,))],
            )
            h1 = rest[0] if rest else h1
            first_slab += slabs
    return result


def solution(mesh):
    return jax.shard_map(
        per_device,
        mesh=mesh,
        in_specs=(P(AXES, None), P(AXES, None, None, None), P(AXES, None), P()),
        out_specs=P(AXES, None),
        check_vma=False,
    )
```

```python
import functools

import jax
import jax.numpy as jnp
from jax import lax
from jax.experimental import pallas as pl
from jax.experimental.pallas import tpu as pltpu
from jax.sharding import PartitionSpec as P

AXES = ("row", "col")
B = 128
PAIR = 2 * B
HEAD = 5 * B + 16
LIMIT = pltpu.CompilerParams(vmem_limit_bytes=16 * 1024 * 1024)
FREE = pl.CostEstimate(flops=0, bytes_accessed=0, transcendentals=0)
TO_X = ((HEAD, 4), (0, 4))
DIRECT = ((HEAD, 0),)
VIA_X = ((0, 4), (0, 4))


def place():
    return lax.axis_index("row") * lax.axis_size("col") + lax.axis_index("col")


def dot(a, b):
    return jnp.dot(a, b, preferred_element_type=jnp.float32)


def turn(block):
    return block.astype(jnp.float32).T.astype(block.dtype)


def grid():
    return (lax.broadcasted_iota(jnp.int32, (B, B), axis) for axis in (0, 1))


def natural(pair, pairs):
    odd = lax.rem(place(), 2)
    return pl.ds(pl.multiple_of(jnp.where(odd == 1, pairs - 1 - pair, pair) * PAIR, PAIR), PAIR)


def pack_kernel(total_blocks, cols_ref, blocks_ref, v_ref, own_ref, *sent):
    x_refs, d_refs = sent[: len(TO_X)], sent[len(TO_X) :]
    here = place()
    odd = lax.rem(here, 2)
    rows_here, slots = blocks_ref.shape[0], blocks_ref.shape[1]
    pairs = rows_here // 2
    first = here * rows_here
    own_ref[...] = jnp.zeros_like(own_ref)
    for r in range(rows_here):
        j, i = r // 2, r % 2
        row = pl.multiple_of(jnp.where(odd == 1, pairs - 1 - j, j) * PAIR + i * B, B)
        for k in range(slots):
            offset = lax.rem(cols_ref[r, k] - (first + r) + 2 + total_blocks, total_blocks)
            at = offset + i
            turned = (2 - at // 2) * 2 + lax.rem(at, 2)
            col = pl.multiple_of(jnp.where(odd == 1, turned, at) * B, B)
            own_ref[pl.ds(row, B), pl.ds(col, B)] += blocks_ref[r, k]
    last = (pairs - 1) * PAIR
    for out, row, near, mid in ((x_refs[0], last, PAIR, 0), (d_refs[0], 0, PAIR, 2 * PAIR)):
        upper, lower = slice(row, row + B), slice(row + B, row + 2 * B)
        first_block, second = (
            own_ref[rows, near + at : near + at + B].astype(jnp.float32)
            for rows, at in ((upper, 0), (lower, B))
        )
        i, j = grid()
        out[0:B, :] = jnp.where(j >= i, first_block, second).astype(out.dtype)
        diagonal = jnp.sum(jnp.where(i == j, second, 0.0), axis=0, keepdims=True)
        out[5 * B : HEAD, :] = jnp.broadcast_to(diagonal, (HEAD - 5 * B, B)).astype(out.dtype)
        out[B : 2 * B, :] = own_ref[upper, near + B : near + 2 * B]
        out[2 * B : 3 * B, :] = own_ref[upper, mid : mid + B]
        out[3 * B : 4 * B, :] = (
            own_ref[upper, mid + B : mid + 2 * B] + own_ref[lower, mid : mid + B]
        )
        out[4 * B : 5 * B, :] = own_ref[lower, mid + B : mid + 2 * B]
    for refs, layout, edge in ((x_refs, TO_X, pairs - 1), (d_refs, DIRECT + VIA_X, 0)):
        slab = 0
        for ref, (head, slabs) in zip(refs, layout, strict=True):
            for s in range(slabs):
                at = head + s * PAIR
                ref[at : at + PAIR, :] = v_ref[natural(edge, pairs), slab * B : (slab + 1) * B]
                slab += 1


def scales(bounds_ref):
    low, high = bounds_ref[0], bounds_ref[1]
    return 0.5 * (high + low), 0.5 * (high - low)


def core_kernel(bounds_ref, v_ref, own_ref, one_ref, g0_ref, g2_ref, h0_ref, h1_ref, h2_ref):
    pairs = v_ref.shape[0] // PAIR
    center, halfwidth = scales(bounds_ref)
    for at in range(0, v_ref.shape[1], PAIR):
        lanes = slice(at, at + PAIR)
        v0, v1, v2 = (v_ref[natural(j, pairs), lanes] for j in range(3))
        v = jnp.concatenate([v0, v1, v2], axis=0)
        g0_ref[:, lanes] = dot(own_ref[0:PAIR, PAIR:], v[: 2 * PAIR])
        g2_ref[:, lanes] = dot(own_ref[2 * PAIR :, : 2 * PAIR], v[PAIR:])
        image = dot(own_ref[PAIR : 2 * PAIR, :], v)
        one = ((image - center * v1.astype(jnp.float32)) / halfwidth).astype(one_ref.dtype)
        one_ref[:, lanes] = one
        h0_ref[:, lanes] = dot(own_ref[0:PAIR, 2 * PAIR :], one)
        h1_ref[:, lanes] = dot(own_ref[PAIR : 2 * PAIR, PAIR : 2 * PAIR], one)
        h2_ref[:, lanes] = dot(own_ref[2 * PAIR :, 0:PAIR], one)


def halo_kernel(side, own_ref, sent_ref, halo_ref):
    odd = lax.rem(place(), 2)
    halo_ref[...] = jnp.zeros_like(halo_ref)
    if side == 0:
        known, low = own_ref[0:PAIR, 0:PAIR], odd
    else:
        known, low = own_ref[2 * PAIR :, 2 * PAIR :], 1 - odd
    halo_ref[:, 0:PAIR] = turn(known)
    near, far = PAIR, 2 * PAIR
    halves = sent_ref[0:B, :].astype(jnp.float32)
    i, j = grid()
    diagonal = jnp.broadcast_to(sent_ref[5 * B : HEAD, :].astype(jnp.float32)[0:1], (B, B))
    halo_ref[0:B, near : near + B] = jnp.where(j >= i, halves, halves.T).astype(halo_ref.dtype)
    halo_ref[B:PAIR, near + B : near + PAIR] = jnp.where(
        j < i, halves, jnp.where(j > i, halves.T, diagonal)
    ).astype(halo_ref.dtype)
    halo_ref[0:B, near + B : near + PAIR] = sent_ref[B : 2 * B, :]
    halo_ref[B:PAIR, near : near + B] = turn(sent_ref[B : 2 * B, :])
    halo_ref[0:B, far : far + B] = sent_ref[2 * B : 3 * B, :]
    halo_ref[
        pl.ds(pl.multiple_of(low * B, B), B), pl.ds(pl.multiple_of(far + (1 - low) * B, B), B)
    ] = sent_ref[3 * B : 4 * B, :]
    halo_ref[B:PAIR, far + B : far + PAIR] = sent_ref[4 * B : 5 * B, :]


def side_kernel(side, first_slab, layout, bounds_ref, v_ref, own_ref, halo_ref, low_ref, high_ref, *refs):
    near_refs, refs = refs[: len(layout)], refs[len(layout) :]
    if side == 0:
        g_ref, h_ref, h1_ref, h1_out, end_out = refs
    else:
        g_ref, h_ref, h1_ref, one_ref, zero_ref = refs[:5]
        out_ref, end_ref, mid_ref, sems = refs[-4:]
    pairs = v_ref.shape[0] // PAIR
    center, halfwidth = scales(bounds_ref)
    edge = 0 if side == 0 else 2
    rows = slice(edge * PAIR, (edge + 1) * PAIR)
    outward = slice(0, PAIR) if side == 0 else slice(2 * PAIR, 3 * PAIR)
    slabs = [
        near_ref[head + s * PAIR : head + (s + 1) * PAIR, :]
        for near_ref, (head, count) in zip(near_refs, layout, strict=True)
        for s in range(count)
    ]
    width = len(slabs) * B
    all_lanes = slice(first_slab * B, first_slab * B + width)
    copies = []
    if side == 1:
        copies = [
            pltpu.make_async_copy(source, out_ref.at[natural(pair, pairs), all_lanes], sems.at[pair])
            for pair, source in enumerate((zero_ref, mid_ref, end_ref))
        ]
        copies[0].start()
    for at in range(0, width, PAIR):
        lanes = slice(first_slab * B + at, first_slab * B + at + PAIR)
        here = slice(at, at + PAIR)
        near = jnp.concatenate(slabs[at // B : at // B + 2], axis=1)
        v = v_ref[natural(edge, pairs), lanes]
        stack = jnp.concatenate([v, near, low_ref[:, lanes], high_ref[:, lanes]], axis=0)
        v32 = v.astype(jnp.float32)
        image = g_ref[:, lanes] + dot(own_ref[rows, outward], near)
        edge_one = ((image - center * v32) / halfwidth).astype(v.dtype)
        image = dot(halo_ref[...], stack)
        near_one = ((image - center * near.astype(jnp.float32)) / halfwidth).astype(v.dtype)
        h1 = dot(own_ref[PAIR : 2 * PAIR, outward], edge_one)
        if side == 0:
            h1_out[:, here] = h1_ref[:, lanes] + h1
        else:
            h1 += h1_ref[:, here]
            one = one_ref[:, lanes].astype(jnp.float32)
            v1 = v_ref[natural(1, pairs), lanes].astype(jnp.float32)
            mid_ref[:, here] = (2.0 * ((h1 - center * one) / halfwidth) - v1).astype(v.dtype)
        image = h_ref[:, lanes] + (
            dot(own_ref[rows, PAIR : 2 * PAIR], edge_one) + dot(own_ref[rows, outward], near_one)
        )
        end = (2.0 * ((image - center * edge_one.astype(jnp.float32)) / halfwidth) - v32).astype(v.dtype)
        if side == 0:
            end_out[:, here] = end
        else:
            end_ref[:, here] = end
    for copy in copies[1:]:
        copy.start()
    for copy in copies:
        copy.wait()


def whole(ref_space=pltpu.VMEM):
    return pl.BlockSpec(memory_space=ref_space)


def call(body, outs, args, name, aliases=None, scratch=()):
    aliases = aliases or {}

    def in_hbm(out):
        return isinstance(out, jax.ShapeDtypeStruct)

    spaces = [
        pltpu.SMEM
        if a.size < 1024
        else pl.ANY
        if i in aliases and in_hbm(outs[aliases[i]])
        else pltpu.VMEM
        for i, a in enumerate(args)
    ]
    return pl.pallas_call(
        body,
        out_shape=outs,
        in_specs=[whole(space) for space in spaces],
        out_specs=[whole(pl.ANY if in_hbm(out) else pltpu.VMEM) for out in outs],
        scratch_shapes=scratch,
        input_output_aliases=aliases,
        compiler_params=LIMIT,
        cost_estimate=FREE,
        name=name,
    )(
        *(
            pltpu.with_memory_space_constraint(a, pltpu.VMEM) if space == pltpu.VMEM else a
            for a, space in zip(args, spaces, strict=True)
        )
    )


def after(token, value):
    return lax.optimization_barrier((token, value))


def per_device(vectors, ham_blocks, ham_columns, bounds):
    rows, vec_width = vectors.shape
    rows_here = ham_blocks.shape[0]
    ring = lax.axis_size(AXES)
    dtype = vectors.dtype
    over_x = [(i, i ^ 1) for i in range(ring)]
    direct = [(i, (i + 1) % ring if i % 2 else (i - 1) % ring) for i in range(ring)]
    onward = [(i, (i - 2) % ring if i % 2 else (i + 2) % ring) for i in range(ring)]

    def send(part, perm):
        return lax.ppermute(part, AXES, perm)

    middle = [lax.slice_in_dim(vectors, rows // 2 + at, rows // 2 + at + B, axis=0) for at in (-B, 0)]
    own, *parts = call(
        functools.partial(pack_kernel, ring * rows_here),
        [pltpu.VMEM((rows, 3 * PAIR), dtype)]
        + [
            pltpu.VMEM((head + slabs * PAIR, B), dtype) for head, slabs in TO_X + DIRECT + VIA_X
        ],
        [ham_columns, ham_blocks, vectors],
        "pack",
    )
    to_x, parts = parts[: len(TO_X)], parts[len(TO_X) :]
    to_d, via_x = parts[: len(DIRECT)], parts[len(DIRECT) :]

    far_x = [send(part, over_x) for part in middle]
    near_d = [send(part, direct) for part in to_d]
    far_x[0], via_x[0] = after(far_x[0], via_x[0])
    far_x[1], via_x[1] = after(far_x[1], via_x[1])
    far_d = [send(part, onward) for part in far_x]
    passing = [send(part, over_x) for part in via_x]
    far_d[0], to_x[0] = after(far_d[0], to_x[0])
    near_d[0], to_x[0] = after(near_d[0], to_x[0])
    passing[0], to_x[0] = after(passing[0], to_x[0])
    far_d[1], passing[1] = after(far_d[1], passing[1])
    passing[1], to_x[1] = after(passing[1], to_x[1])
    near_d += [send(part, onward) for part in passing]
    near_x = [send(part, over_x) for part in to_x]

    wide = lambda kind: pltpu.VMEM((PAIR, vec_width), kind)
    one, g0, g2, h0, h1, h2 = call(
        core_kernel, [wide(dtype)] + [wide(jnp.float32)] * 5, [bounds, vectors, own], "core"
    )
    band = [pltpu.VMEM((PAIR, 3 * PAIR), dtype)]
    (halo_d,) = call(functools.partial(halo_kernel, 0), band, [own, near_d[0]], "halo_d")
    result = None
    first_slab = 0
    for c, (head, slabs) in enumerate(TO_X):
        if c == 0:
            layout, near = (DIRECT + VIA_X)[:2], near_d[:2]
        else:
            layout, near = VIA_X[c : c + 1], near_d[c + 1 : c + 2]
            near[0], result = after(near[0], result)
        chunk = lambda kind, slabs=slabs: pltpu.VMEM((PAIR, slabs * B), kind)
        mid, zero = call(
            functools.partial(side_kernel, 0, first_slab, layout),
            [chunk(jnp.float32), chunk(dtype)],
            [bounds, vectors, own, halo_d, *far_d, *near, g0, h0, h1],
            "side_d",
        )
        near_x[c], zero = after(near_x[c], zero)
        if c == 0:
            (halo_x,) = call(functools.partial(halo_kernel, 1), band, [own, near_x[0]], "halo_x")
        args = [bounds, vectors, own, halo_x, *far_x, near_x[c], g2, h2, mid, one, zero]
        aliases = {}
        if result is not None:
            aliases[len(args)] = 0
            args.append(result)
        (result,) = call(
            functools.partial(side_kernel, 1, first_slab, ((head, slabs),)),
            [jax.ShapeDtypeStruct((rows, vec_width), dtype)],
            args,
            "side_x",
            aliases=aliases,
            scratch=[chunk(dtype)] * 2 + [pltpu.SemaphoreType.DMA((3,))],
        )
        first_slab += slabs
    return result


def solution(mesh):
    return jax.shard_map(
        per_device,
        mesh=mesh,
        in_specs=(P(AXES, None), P(AXES, None, None, None), P(AXES, None), P()),
        out_specs=P(AXES, None),
        check_vma=False,
    )
```

```python
import functools

import jax
import jax.numpy as jnp
from jax import lax
from jax.experimental import pallas as pl
from jax.experimental.pallas import tpu as pltpu
from jax.sharding import PartitionSpec as P

AXES = ("row", "col")
B = 128
PAIR = 2 * B
STEP = 4 * B
HEAD = 5 * B + 16
LIMIT = pltpu.CompilerParams(vmem_limit_bytes=16 * 1024 * 1024)
FREE = pl.CostEstimate(flops=0, bytes_accessed=0, transcendentals=0)
TO_X = ((HEAD, 4), (0, 4))
DIRECT = ((HEAD, 0),)
VIA_X = ((0, 4), (0, 4))


def place():
    return lax.axis_index("row") * lax.axis_size("col") + lax.axis_index("col")


def dot(a, b):
    return jnp.dot(a, b, preferred_element_type=jnp.float32)


def turn(block):
    return block.astype(jnp.float32).T.astype(block.dtype)


def grid():
    return (lax.broadcasted_iota(jnp.int32, (B, B), axis) for axis in (0, 1))


def natural(pair, pairs):
    odd = lax.rem(place(), 2)
    return pl.ds(pl.multiple_of(jnp.where(odd == 1, pairs - 1 - pair, pair) * PAIR, PAIR), PAIR)


def pack_kernel(total_blocks, cols_ref, bounds_ref, blocks_ref, v_ref, scales_ref, own_ref, *sent):
    low, high = bounds_ref[0], bounds_ref[1]
    scales_ref[0:1, :] = jnp.full((1, B), 0.5 * (high + low), jnp.float32)
    scales_ref[1:2, :] = jnp.full((1, B), 0.5 * (high - low), jnp.float32)
    x_refs, d_refs = sent[: len(TO_X)], sent[len(TO_X) :]
    here = place()
    odd = lax.rem(here, 2)
    rows_here, slots = blocks_ref.shape[0], blocks_ref.shape[1]
    pairs = rows_here // 2
    first = here * rows_here
    own_ref[...] = jnp.zeros_like(own_ref)
    for r in range(rows_here):
        j, i = r // 2, r % 2
        row = pl.multiple_of(jnp.where(odd == 1, pairs - 1 - j, j) * PAIR + i * B, B)
        for k in range(slots):
            offset = lax.rem(cols_ref[r, k] - (first + r) + 2 + total_blocks, total_blocks)
            at = offset + i
            turned = (2 - at // 2) * 2 + lax.rem(at, 2)
            col = pl.multiple_of(jnp.where(odd == 1, turned, at) * B, B)
            own_ref[pl.ds(row, B), pl.ds(col, B)] += blocks_ref[r, k]
    last = (pairs - 1) * PAIR
    for out, row, near, mid in ((x_refs[0], last, PAIR, 0), (d_refs[0], 0, PAIR, 2 * PAIR)):
        upper, lower = slice(row, row + B), slice(row + B, row + 2 * B)
        first_block, second = (
            own_ref[rows, near + at : near + at + B].astype(jnp.float32)
            for rows, at in ((upper, 0), (lower, B))
        )
        i, j = grid()
        out[0:B, :] = jnp.where(j >= i, first_block, second).astype(out.dtype)
        diagonal = jnp.sum(jnp.where(i == j, second, 0.0), axis=0, keepdims=True)
        out[5 * B : HEAD, :] = jnp.broadcast_to(diagonal, (HEAD - 5 * B, B)).astype(out.dtype)
        out[B : 2 * B, :] = own_ref[upper, near + B : near + 2 * B]
        out[2 * B : 3 * B, :] = own_ref[upper, mid : mid + B]
        out[3 * B : 4 * B, :] = (
            own_ref[upper, mid + B : mid + 2 * B] + own_ref[lower, mid : mid + B]
        )
        out[4 * B : 5 * B, :] = own_ref[lower, mid + B : mid + 2 * B]
    for refs, layout, edge in ((x_refs, TO_X, pairs - 1), (d_refs, DIRECT + VIA_X, 0)):
        slab = 0
        for ref, (head, slabs) in zip(refs, layout, strict=True):
            for s in range(slabs):
                at = head + s * PAIR
                ref[at : at + PAIR, :] = v_ref[natural(edge, pairs), slab * B : (slab + 1) * B]
                slab += 1


def scales(scales_ref):
    return scales_ref[0:1, 0:1], scales_ref[1:2, 0:1]


def core_kernel(scales_ref, v_ref, own_ref, one_ref, g0_ref, g2_ref, h0_ref, h1_ref, h2_ref):
    pairs = v_ref.shape[0] // PAIR
    center, halfwidth = scales(scales_ref)
    for at in range(0, v_ref.shape[1], STEP):
        lanes = slice(at, at + STEP)
        v0, v1, v2 = (v_ref[natural(j, pairs), lanes] for j in range(3))
        v = jnp.concatenate([v0, v1, v2], axis=0)
        g0_ref[:, lanes] = dot(own_ref[0:PAIR, PAIR:], v[: 2 * PAIR])
        g2_ref[:, lanes] = dot(own_ref[2 * PAIR :, : 2 * PAIR], v[PAIR:])
        image = dot(own_ref[PAIR : 2 * PAIR, :], v)
        one = ((image - center * v1.astype(jnp.float32)) / halfwidth).astype(one_ref.dtype)
        one_ref[:, lanes] = one
        h0_ref[:, lanes] = dot(own_ref[0:PAIR, 2 * PAIR :], one)
        h1_ref[:, lanes] = dot(own_ref[PAIR : 2 * PAIR, PAIR : 2 * PAIR], one)
        h2_ref[:, lanes] = dot(own_ref[2 * PAIR :, 0:PAIR], one)


def halo_kernel(side, own_ref, sent_ref, halo_ref):
    odd = lax.rem(place(), 2)
    halo_ref[...] = jnp.zeros_like(halo_ref)
    if side == 0:
        known, low = own_ref[0:PAIR, 0:PAIR], odd
    else:
        known, low = own_ref[2 * PAIR :, 2 * PAIR :], 1 - odd
    halo_ref[:, 0:PAIR] = turn(known)
    near, far = PAIR, 2 * PAIR
    halves = sent_ref[0:B, :].astype(jnp.float32)
    i, j = grid()
    diagonal = jnp.broadcast_to(sent_ref[5 * B : HEAD, :].astype(jnp.float32)[0:1], (B, B))
    halo_ref[0:B, near : near + B] = jnp.where(j >= i, halves, halves.T).astype(halo_ref.dtype)
    halo_ref[B:PAIR, near + B : near + PAIR] = jnp.where(
        j < i, halves, jnp.where(j > i, halves.T, diagonal)
    ).astype(halo_ref.dtype)
    halo_ref[0:B, near + B : near + PAIR] = sent_ref[B : 2 * B, :]
    halo_ref[B:PAIR, near : near + B] = turn(sent_ref[B : 2 * B, :])
    halo_ref[0:B, far : far + B] = sent_ref[2 * B : 3 * B, :]
    halo_ref[
        pl.ds(pl.multiple_of(low * B, B), B), pl.ds(pl.multiple_of(far + (1 - low) * B, B), B)
    ] = sent_ref[3 * B : 4 * B, :]
    halo_ref[B:PAIR, far + B : far + PAIR] = sent_ref[4 * B : 5 * B, :]


def side_kernel(side, first_slab, layout, scales_ref, v_ref, own_ref, halo_ref, low_ref, high_ref, *refs):
    near_refs, refs = refs[: len(layout)], refs[len(layout) :]
    if side == 0:
        g_ref, h_ref, h1_ref, h1_out, end_out = refs
    else:
        g_ref, h_ref, h1_ref, one_ref, zero_ref = refs[:5]
        out_ref, end_ref, mid_ref, sems = refs[-4:]
    pairs = v_ref.shape[0] // PAIR
    center, halfwidth = scales(scales_ref)
    edge = 0 if side == 0 else 2
    rows = slice(edge * PAIR, (edge + 1) * PAIR)
    outward = slice(0, PAIR) if side == 0 else slice(2 * PAIR, 3 * PAIR)
    slabs = [
        near_ref[head + s * PAIR : head + (s + 1) * PAIR, :]
        for near_ref, (head, count) in zip(near_refs, layout, strict=True)
        for s in range(count)
    ]
    width = len(slabs) * B
    all_lanes = slice(first_slab * B, first_slab * B + width)
    copies = []
    if side == 1:
        copies = [
            pltpu.make_async_copy(source, out_ref.at[natural(pair, pairs), all_lanes], sems.at[pair])
            for pair, source in enumerate((zero_ref, mid_ref, end_ref))
        ]
        copies[0].start()
    for at in range(0, width, STEP):
        to = min(at + STEP, width)
        lanes = slice(first_slab * B + at, first_slab * B + to)
        here = slice(at, to)
        near = jnp.concatenate(slabs[at // B : to // B], axis=1)
        v = v_ref[natural(edge, pairs), lanes]
        others = jnp.concatenate([v, low_ref[:, lanes], high_ref[:, lanes]], axis=0)
        v32 = v.astype(jnp.float32)
        by_near = dot(jnp.concatenate([own_ref[rows, outward], halo_ref[:, PAIR : 2 * PAIR]], axis=0), near)
        image = g_ref[:, lanes] + by_near[:PAIR]
        edge_one = ((image - center * v32) / halfwidth).astype(v.dtype)
        image = by_near[PAIR:] + dot(
            jnp.concatenate([halo_ref[:, :PAIR], halo_ref[:, 2 * PAIR :]], axis=1), others
        )
        near_one = ((image - center * near.astype(jnp.float32)) / halfwidth).astype(v.dtype)
        by_edge = dot(
            jnp.concatenate([own_ref[PAIR : 2 * PAIR, outward], own_ref[rows, PAIR : 2 * PAIR]], axis=0),
            edge_one,
        )
        h1 = by_edge[:PAIR]
        if side == 0:
            h1_out[:, here] = h1_ref[:, lanes] + h1
        else:
            h1 += h1_ref[:, here]
            one = one_ref[:, lanes].astype(jnp.float32)
            v1 = v_ref[natural(1, pairs), lanes].astype(jnp.float32)
            mid_ref[:, here] = (2.0 * ((h1 - center * one) / halfwidth) - v1).astype(v.dtype)
        image = h_ref[:, lanes] + (by_edge[PAIR:] + dot(own_ref[rows, outward], near_one))
        end = (2.0 * ((image - center * edge_one.astype(jnp.float32)) / halfwidth) - v32).astype(v.dtype)
        if side == 0:
            end_out[:, here] = end
        else:
            end_ref[:, here] = end
    for copy in copies[1:]:
        copy.start()
    for copy in copies:
        copy.wait()


def whole(ref_space=pltpu.VMEM):
    return pl.BlockSpec(memory_space=ref_space)


def call(body, outs, args, name, aliases=None, scratch=()):
    aliases = aliases or {}

    def in_hbm(out):
        return isinstance(out, jax.ShapeDtypeStruct)

    spaces = [
        pltpu.SMEM
        if a.size < 1024
        else pl.ANY
        if i in aliases and in_hbm(outs[aliases[i]])
        else pltpu.VMEM
        for i, a in enumerate(args)
    ]
    return pl.pallas_call(
        body,
        out_shape=outs,
        in_specs=[whole(space) for space in spaces],
        out_specs=[whole(pl.ANY if in_hbm(out) else pltpu.VMEM) for out in outs],
        scratch_shapes=scratch,
        input_output_aliases=aliases,
        compiler_params=LIMIT,
        cost_estimate=FREE,
        name=name,
    )(
        *(
            pltpu.with_memory_space_constraint(a, pltpu.VMEM) if space == pltpu.VMEM else a
            for a, space in zip(args, spaces, strict=True)
        )
    )


def after(token, value):
    return lax.optimization_barrier((token, value))


def per_device(vectors, ham_blocks, ham_columns, bounds):
    rows, vec_width = vectors.shape
    rows_here = ham_blocks.shape[0]
    ring = lax.axis_size(AXES)
    dtype = vectors.dtype
    over_x = [(i, i ^ 1) for i in range(ring)]
    direct = [(i, (i + 1) % ring if i % 2 else (i - 1) % ring) for i in range(ring)]
    onward = [(i, (i - 2) % ring if i % 2 else (i + 2) % ring) for i in range(ring)]

    def send(part, perm):
        return lax.ppermute(part, AXES, perm)

    low = lax.slice_in_dim(vectors, rows // 2 - B, rows // 2, axis=0)
    low, rest = after(low, vectors)
    middle = [low, lax.slice_in_dim(rest, rows // 2, rows // 2 + B, axis=0)]
    scale, own, *parts = call(
        functools.partial(pack_kernel, ring * rows_here),
        [pltpu.VMEM((8, B), jnp.float32), pltpu.VMEM((rows, 3 * PAIR), dtype)]
        + [
            pltpu.VMEM((head + slabs * PAIR, B), dtype) for head, slabs in TO_X + DIRECT + VIA_X
        ],
        [ham_columns, bounds, ham_blocks, rest],
        "pack",
    )
    to_x, parts = parts[: len(TO_X)], parts[len(TO_X) :]
    to_d, via_x = parts[: len(DIRECT)], parts[len(DIRECT) :]

    far_x = [send(part, over_x) for part in middle]
    near_d = [send(part, direct) for part in to_d]
    far_x[0], via_x[0] = after(far_x[0], via_x[0])
    far_x[1], via_x[1] = after(far_x[1], via_x[1])
    far_d = [send(part, onward) for part in far_x]
    passing = [send(part, over_x) for part in via_x]
    far_d[0], to_x[0] = after(far_d[0], to_x[0])
    near_d[0], to_x[0] = after(near_d[0], to_x[0])
    passing[0], to_x[0] = after(passing[0], to_x[0])
    far_d[1], passing[1] = after(far_d[1], passing[1])
    passing[1], to_x[1] = after(passing[1], to_x[1])
    near_d += [send(part, onward) for part in passing]
    near_x = [send(part, over_x) for part in to_x]

    wide = lambda kind: pltpu.VMEM((PAIR, vec_width), kind)
    one, g0, g2, h0, h1, h2 = call(
        core_kernel, [wide(dtype)] + [wide(jnp.float32)] * 5, [scale, vectors, own], "core"
    )
    band = [pltpu.VMEM((PAIR, 3 * PAIR), dtype)]
    (halo_d,) = call(functools.partial(halo_kernel, 0), band, [own, near_d[0]], "halo_d")
    result = None
    first_slab = 0
    for c, (head, slabs) in enumerate(TO_X):
        if c == 0:
            layout, near = (DIRECT + VIA_X)[:2], near_d[:2]
        else:
            layout, near = VIA_X[c : c + 1], near_d[c + 1 : c + 2]
            near[0], result = after(near[0], result)
        chunk = lambda kind, slabs=slabs: pltpu.VMEM((PAIR, slabs * B), kind)
        mid, zero = call(
            functools.partial(side_kernel, 0, first_slab, layout),
            [chunk(jnp.float32), chunk(dtype)],
            [scale, vectors, own, halo_d, *far_d, *near, g0, h0, h1],
            "side_d",
        )
        near_x[c], zero = after(near_x[c], zero)
        if c == 0:
            (halo_x,) = call(functools.partial(halo_kernel, 1), band, [own, near_x[0]], "halo_x")
        args = [scale, vectors, own, halo_x, *far_x, near_x[c], g2, h2, mid, one, zero]
        aliases = {}
        if result is not None:
            aliases[len(args)] = 0
            args.append(result)
        (result,) = call(
            functools.partial(side_kernel, 1, first_slab, ((head, slabs),)),
            [jax.ShapeDtypeStruct((rows, vec_width), dtype)],
            args,
            "side_x",
            aliases=aliases,
            scratch=[chunk(dtype)] * 2 + [pltpu.SemaphoreType.DMA((3,))],
        )
        first_slab += slabs
    return result


def solution(mesh):
    return jax.shard_map(
        per_device,
        mesh=mesh,
        in_specs=(P(AXES, None), P(AXES, None, None, None), P(AXES, None), P()),
        out_specs=P(AXES, None),
        check_vma=False,
    )
```

```python
import functools

import jax
import jax.numpy as jnp
from jax import lax
from jax.experimental import pallas as pl
from jax.experimental.pallas import tpu as pltpu
from jax.sharding import PartitionSpec as P

AXES = ("row", "col")
B = 128
PAIR = 2 * B
STEP = 4 * B
HEAD = 5 * B + 16
LIMIT = pltpu.CompilerParams(vmem_limit_bytes=16 * 1024 * 1024)
FREE = pl.CostEstimate(flops=0, bytes_accessed=0, transcendentals=0)
TO_X = ((HEAD, 4), (0, 4), )
DIRECT = ((HEAD, 0),)
VIA_X = ((0, 4), (0, 4))


def place():
    return lax.axis_index("row") * lax.axis_size("col") + lax.axis_index("col")


def dot(a, b):
    return jnp.dot(a, b, preferred_element_type=jnp.float32)


def turn(block):
    return block.astype(jnp.float32).T.astype(block.dtype)


def grid():
    return (lax.broadcasted_iota(jnp.int32, (B, B), axis) for axis in (0, 1))


def natural(pair, pairs):
    odd = lax.rem(place(), 2)
    return pl.ds(pl.multiple_of(jnp.where(odd == 1, pairs - 1 - pair, pair) * PAIR, PAIR), PAIR)


def pack_kernel(total_blocks, cols_ref, bounds_ref, blocks_ref, v_ref, scales_ref, own_ref, *sent):
    low, high = bounds_ref[0], bounds_ref[1]
    scales_ref[0:1, :] = jnp.full((1, B), 0.5 * (high + low), jnp.float32)
    scales_ref[1:2, :] = jnp.full((1, B), 0.5 * (high - low), jnp.float32)
    x_refs, d_refs = sent[: len(TO_X)], sent[len(TO_X) :]
    here = place()
    odd = lax.rem(here, 2)
    rows_here, slots = blocks_ref.shape[0], blocks_ref.shape[1]
    pairs = rows_here // 2
    first = here * rows_here
    own_ref[...] = jnp.zeros_like(own_ref)
    for r in range(rows_here):
        j, i = r // 2, r % 2
        row = pl.multiple_of(jnp.where(odd == 1, pairs - 1 - j, j) * PAIR + i * B, B)
        for k in range(slots):
            offset = lax.rem(cols_ref[r, k] - (first + r) + 2 + total_blocks, total_blocks)
            at = offset + i
            turned = (2 - at // 2) * 2 + lax.rem(at, 2)
            col = pl.multiple_of(jnp.where(odd == 1, turned, at) * B, B)
            own_ref[pl.ds(row, B), pl.ds(col, B)] += blocks_ref[r, k]
    last = (pairs - 1) * PAIR
    for out, row, near, mid in ((x_refs[0], last, PAIR, 0), (d_refs[0], 0, PAIR, 2 * PAIR)):
        upper, lower = slice(row, row + B), slice(row + B, row + 2 * B)
        first_block, second = (
            own_ref[rows, near + at : near + at + B].astype(jnp.float32)
            for rows, at in ((upper, 0), (lower, B))
        )
        i, j = grid()
        out[0:B, :] = jnp.where(j >= i, first_block, second).astype(out.dtype)
        diagonal = jnp.sum(jnp.where(i == j, second, 0.0), axis=0, keepdims=True)
        out[5 * B : HEAD, :] = jnp.broadcast_to(diagonal, (HEAD - 5 * B, B)).astype(out.dtype)
        out[B : 2 * B, :] = own_ref[upper, near + B : near + 2 * B]
        out[2 * B : 3 * B, :] = own_ref[upper, mid : mid + B]
        out[3 * B : 4 * B, :] = (
            own_ref[upper, mid + B : mid + 2 * B] + own_ref[lower, mid : mid + B]
        )
        out[4 * B : 5 * B, :] = own_ref[lower, mid + B : mid + 2 * B]
    for refs, layout, edge in ((x_refs, TO_X, pairs - 1), (d_refs, DIRECT + VIA_X, 0)):
        slab = 0
        for ref, (head, slabs) in zip(refs, layout, strict=True):
            for s in range(slabs):
                at = head + s * PAIR
                ref[at : at + PAIR, :] = v_ref[natural(edge, pairs), slab * B : (slab + 1) * B]
                slab += 1


def scales(scales_ref):
    return scales_ref[0:1, 0:1], scales_ref[1:2, 0:1]


def core_kernel(scales_ref, v_ref, own_ref, one_ref, g0_ref, g2_ref, h0_ref, h1_ref, h2_ref):
    pairs = v_ref.shape[0] // PAIR
    center, halfwidth = scales(scales_ref)
    for at in range(0, v_ref.shape[1], STEP):
        lanes = slice(at, at + STEP)
        v0, v1, v2 = (v_ref[natural(j, pairs), lanes] for j in range(3))
        v = jnp.concatenate([v0, v1, v2], axis=0)
        g0_ref[:, lanes] = dot(own_ref[0:PAIR, PAIR:], v[: 2 * PAIR])
        g2_ref[:, lanes] = dot(own_ref[2 * PAIR :, : 2 * PAIR], v[PAIR:])
        image = dot(own_ref[PAIR : 2 * PAIR, :], v)
        one = ((image - center * v1.astype(jnp.float32)) / halfwidth).astype(one_ref.dtype)
        one_ref[:, lanes] = one
        h0_ref[:, lanes] = dot(own_ref[0:PAIR, 2 * PAIR :], one)
        h1_ref[:, lanes] = dot(own_ref[PAIR : 2 * PAIR, PAIR : 2 * PAIR], one)
        h2_ref[:, lanes] = dot(own_ref[2 * PAIR :, 0:PAIR], one)


def halo_kernel(side, own_ref, sent_ref, halo_ref):
    odd = lax.rem(place(), 2)
    halo_ref[...] = jnp.zeros_like(halo_ref)
    if side == 0:
        known, low = own_ref[0:PAIR, 0:PAIR], odd
    else:
        known, low = own_ref[2 * PAIR :, 2 * PAIR :], 1 - odd
    halo_ref[:, 0:PAIR] = turn(known)
    near, far = PAIR, 2 * PAIR
    halves = sent_ref[0:B, :].astype(jnp.float32)
    i, j = grid()
    diagonal = jnp.broadcast_to(sent_ref[5 * B : HEAD, :].astype(jnp.float32)[0:1], (B, B))
    halo_ref[0:B, near : near + B] = jnp.where(j >= i, halves, halves.T).astype(halo_ref.dtype)
    halo_ref[B:PAIR, near + B : near + PAIR] = jnp.where(
        j < i, halves, jnp.where(j > i, halves.T, diagonal)
    ).astype(halo_ref.dtype)
    halo_ref[0:B, near + B : near + PAIR] = sent_ref[B : 2 * B, :]
    halo_ref[B:PAIR, near : near + B] = turn(sent_ref[B : 2 * B, :])
    halo_ref[0:B, far : far + B] = sent_ref[2 * B : 3 * B, :]
    halo_ref[
        pl.ds(pl.multiple_of(low * B, B), B), pl.ds(pl.multiple_of(far + (1 - low) * B, B), B)
    ] = sent_ref[3 * B : 4 * B, :]
    halo_ref[B:PAIR, far + B : far + PAIR] = sent_ref[4 * B : 5 * B, :]


def side_kernel(side, first_slab, held_slab, layout, scales_ref, v_ref, own_ref, halo_ref, low_ref, high_ref, *refs):
    near_refs, refs = refs[: len(layout)], refs[len(layout) :]
    if side == 0:
        g_ref, h_ref, h1_ref, h1_out, end_out = refs
    else:
        g_ref, h_ref, h1_ref, one_ref, zero_ref = refs[:5]
        out_ref, end_ref, mid_ref, sems = refs[-4:]
    pairs = v_ref.shape[0] // PAIR
    center, halfwidth = scales(scales_ref)
    edge = 0 if side == 0 else 2
    rows = slice(edge * PAIR, (edge + 1) * PAIR)
    outward = slice(0, PAIR) if side == 0 else slice(2 * PAIR, 3 * PAIR)
    slabs = [
        near_ref[head + s * PAIR : head + (s + 1) * PAIR, :]
        for near_ref, (head, count) in zip(near_refs, layout, strict=True)
        for s in range(count)
    ]
    width = len(slabs) * B
    all_lanes = slice(first_slab * B, first_slab * B + width)
    copies = []
    if side == 1:
        copies = [
            pltpu.make_async_copy(source, out_ref.at[natural(pair, pairs), all_lanes], sems.at[pair])
            for pair, source in ((1, mid_ref), (2, end_ref))
        ]
        if held_slab == first_slab:
            held = slice(held_slab * B, held_slab * B + zero_ref.shape[1])
            copies.insert(
                0, pltpu.make_async_copy(zero_ref, out_ref.at[natural(0, pairs), held], sems.at[0])
            )
            copies[0].start()
    for at in range(0, width, STEP):
        to = min(at + STEP, width)
        lanes = slice(first_slab * B + at, first_slab * B + to)
        here = slice(at, to)
        held = slice((first_slab - held_slab) * B + at, (first_slab - held_slab) * B + to)
        near = jnp.concatenate(slabs[at // B : to // B], axis=1)
        v = v_ref[natural(edge, pairs), lanes]
        others = jnp.concatenate([v, low_ref[:, lanes], high_ref[:, lanes]], axis=0)
        v32 = v.astype(jnp.float32)
        by_near = dot(jnp.concatenate([own_ref[rows, outward], halo_ref[:, PAIR : 2 * PAIR]], axis=0), near)
        image = g_ref[:, lanes] + by_near[:PAIR]
        edge_one = ((image - center * v32) / halfwidth).astype(v.dtype)
        image = by_near[PAIR:] + dot(
            jnp.concatenate([halo_ref[:, :PAIR], halo_ref[:, 2 * PAIR :]], axis=1), others
        )
        near_one = ((image - center * near.astype(jnp.float32)) / halfwidth).astype(v.dtype)
        by_edge = dot(
            jnp.concatenate([own_ref[PAIR : 2 * PAIR, outward], own_ref[rows, PAIR : 2 * PAIR]], axis=0),
            edge_one,
        )
        h1 = by_edge[:PAIR]
        if side == 0:
            h1_out[:, here] = h1_ref[:, lanes] + h1
        else:
            h1 += h1_ref[:, held]
            one = one_ref[:, lanes].astype(jnp.float32)
            v1 = v_ref[natural(1, pairs), lanes].astype(jnp.float32)
            mid_ref[:, here] = (2.0 * ((h1 - center * one) / halfwidth) - v1).astype(v.dtype)
        image = h_ref[:, lanes] + (by_edge[PAIR:] + dot(own_ref[rows, outward], near_one))
        end = (2.0 * ((image - center * edge_one.astype(jnp.float32)) / halfwidth) - v32).astype(v.dtype)
        if side == 0:
            end_out[:, here] = end
        else:
            end_ref[:, here] = end
    for copy in copies[-2:]:
        copy.start()
    for copy in copies:
        copy.wait()


def whole(ref_space=pltpu.VMEM):
    return pl.BlockSpec(memory_space=ref_space)


def call(body, outs, args, name, aliases=None, scratch=()):
    aliases = aliases or {}

    def in_hbm(out):
        return isinstance(out, jax.ShapeDtypeStruct)

    spaces = [
        pltpu.SMEM
        if a.size < 1024
        else pl.ANY
        if i in aliases and in_hbm(outs[aliases[i]])
        else pltpu.VMEM
        for i, a in enumerate(args)
    ]
    return pl.pallas_call(
        body,
        out_shape=outs,
        in_specs=[whole(space) for space in spaces],
        out_specs=[whole(pl.ANY if in_hbm(out) else pltpu.VMEM) for out in outs],
        scratch_shapes=scratch,
        input_output_aliases=aliases,
        compiler_params=LIMIT,
        cost_estimate=FREE,
        name=name,
    )(
        *(
            pltpu.with_memory_space_constraint(a, pltpu.VMEM) if space == pltpu.VMEM else a
            for a, space in zip(args, spaces, strict=True)
        )
    )


def after(token, value):
    return lax.optimization_barrier((token, value))


def per_device(vectors, ham_blocks, ham_columns, bounds):
    rows, vec_width = vectors.shape
    rows_here = ham_blocks.shape[0]
    ring = lax.axis_size(AXES)
    dtype = vectors.dtype
    over_x = [(i, i ^ 1) for i in range(ring)]
    direct = [(i, (i + 1) % ring if i % 2 else (i - 1) % ring) for i in range(ring)]
    onward = [(i, (i - 2) % ring if i % 2 else (i + 2) % ring) for i in range(ring)]

    def send(part, perm):
        return lax.ppermute(part, AXES, perm)

    low = lax.slice_in_dim(vectors, rows // 2 - B, rows // 2, axis=0)
    low, rest = after(low, vectors)
    middle = [low, lax.slice_in_dim(rest, rows // 2, rows // 2 + B, axis=0)]
    scale, own, *parts = call(
        functools.partial(pack_kernel, ring * rows_here),
        [pltpu.VMEM((8, B), jnp.float32), pltpu.VMEM((rows, 3 * PAIR), dtype)]
        + [
            pltpu.VMEM((head + slabs * PAIR, B), dtype) for head, slabs in TO_X + DIRECT + VIA_X
        ],
        [ham_columns, bounds, ham_blocks, rest],
        "pack",
    )
    to_x, parts = parts[: len(TO_X)], parts[len(TO_X) :]
    to_d, via_x = parts[: len(DIRECT)], parts[len(DIRECT) :]

    far_x = [send(part, over_x) for part in middle]
    near_d = [send(part, direct) for part in to_d]
    far_x[1], via_x[1] = after(far_x[1], via_x[1])
    far_d = [send(part, onward) for part in far_x]
    passing = [send(part, over_x) for part in via_x]
    far_d[0], passing[0] = after(far_d[0], passing[0])
    far_d[1], passing[1] = after(far_d[1], passing[1])
    near_d += [send(part, onward) for part in passing]
    passing[0], to_x[0] = after(passing[0], to_x[0])
    near_d[0], to_x[0] = after(near_d[0], to_x[0])
    passing[1], to_x[1] = after(passing[1], to_x[1])

    wide = lambda kind: pltpu.VMEM((PAIR, vec_width), kind)
    one, g0, g2, h0, h1, h2 = call(
        core_kernel, [wide(dtype)] + [wide(jnp.float32)] * 5, [scale, vectors, own], "core"
    )
    band = [pltpu.VMEM((PAIR, 3 * PAIR), dtype)]
    (halo_d,) = call(functools.partial(halo_kernel, 0), band, [own, near_d[0]], "halo_d")
    result, mid, zero = None, None, None
    first_slab, held_slab, c = 0, 0, -1
    for part, (head, slabs) in zip(to_x, TO_X, strict=True):
        near = None if first_slab else send(part, over_x)
        if mid is None or first_slab * B == held_slab * B + mid.shape[1]:
            c += 1
            held_slab = first_slab
            layout, near_c = ((DIRECT + VIA_X)[:2], near_d[:2]) if c == 0 else (VIA_X[c : c + 1], near_d[c + 1 : c + 2])
            if result is not None:
                near_c[0], result = after(near_c[0], result)
            width = sum(count for _, count in layout) * B
            mid, zero = call(
                functools.partial(side_kernel, 0, first_slab, held_slab, layout),
                [pltpu.VMEM((PAIR, width), jnp.float32), pltpu.VMEM((PAIR, width), dtype)],
                [scale, vectors, own, halo_d, *far_d, *near_c, g0, h0, h1],
                "side_d",
            )
        if near is None:
            near = send(part, over_x)
        if held_slab == first_slab:
            near, zero = after(near, zero)
        else:
            near, result = after(near, result)
        if result is None:
            (halo_x,) = call(functools.partial(halo_kernel, 1), band, [own, near], "halo_x")
        args = [scale, vectors, own, halo_x, *far_x, near, g2, h2, mid, one, zero]
        aliases = {}
        if result is not None:
            aliases[len(args)] = 0
            args.append(result)
        (result,) = call(
            functools.partial(side_kernel, 1, first_slab, held_slab, ((head, slabs),)),
            [jax.ShapeDtypeStruct((rows, vec_width), dtype)],
            args,
            "side_x",
            aliases=aliases,
            scratch=[pltpu.VMEM((PAIR, slabs * B), dtype)] * 2 + [pltpu.SemaphoreType.DMA((3,))],
        )
        first_slab += slabs
    return result


def solution(mesh):
    return jax.shard_map(
        per_device,
        mesh=mesh,
        in_specs=(P(AXES, None), P(AXES, None, None, None), P(AXES, None), P()),
        out_specs=P(AXES, None),
        check_vma=False,
    )
```

```python
import functools

import jax
import jax.numpy as jnp
from jax import lax
from jax.experimental import pallas as pl
from jax.experimental.pallas import tpu as pltpu
from jax.sharding import PartitionSpec as P

AXES = ("row", "col")
B = 128
PAIR = 2 * B
STEP = 4 * B
HEAD = 5 * B + 16
LIMIT = pltpu.CompilerParams(vmem_limit_bytes=16 * 1024 * 1024)
FREE = pl.CostEstimate(flops=0, bytes_accessed=0, transcendentals=0)
TO_X = ((HEAD, 4), (0, 4), )
DIRECT = ((HEAD, 0),)
VIA_X = ((0, 4), (0, 4))


def place():
    return lax.axis_index("row") * lax.axis_size("col") + lax.axis_index("col")


def dot(a, b):
    return jnp.dot(a, b, preferred_element_type=jnp.float32)


def turn(block):
    return block.astype(jnp.float32).T.astype(block.dtype)


def grid():
    return (lax.broadcasted_iota(jnp.int32, (B, B), axis) for axis in (0, 1))


def natural(pair, pairs):
    odd = lax.rem(place(), 2)
    return pl.ds(pl.multiple_of(jnp.where(odd == 1, pairs - 1 - pair, pair) * PAIR, PAIR), PAIR)


def pack_kernel(total_blocks, cols_ref, bounds_ref, blocks_ref, v_ref, scales_ref, own_ref, *sent):
    low, high = bounds_ref[0], bounds_ref[1]
    scales_ref[0:1, :] = jnp.full((1, B), 0.5 * (high + low), jnp.float32)
    scales_ref[1:2, :] = jnp.full((1, B), 0.5 * (high - low), jnp.float32)
    x_refs, d_refs = sent[: len(TO_X)], sent[len(TO_X) :]
    here = place()
    odd = lax.rem(here, 2)
    rows_here, slots = blocks_ref.shape[0], blocks_ref.shape[1]
    pairs = rows_here // 2
    first = here * rows_here
    own_ref[...] = jnp.zeros_like(own_ref)
    for r in range(rows_here):
        j, i = r // 2, r % 2
        row = pl.multiple_of(jnp.where(odd == 1, pairs - 1 - j, j) * PAIR + i * B, B)
        for k in range(slots):
            offset = lax.rem(cols_ref[r, k] - (first + r) + 2 + total_blocks, total_blocks)
            at = offset + i
            turned = (2 - at // 2) * 2 + lax.rem(at, 2)
            col = pl.multiple_of(jnp.where(odd == 1, turned, at) * B, B)
            own_ref[pl.ds(row, B), pl.ds(col, B)] += blocks_ref[r, k]
    last = (pairs - 1) * PAIR
    for out, row, near, mid in ((x_refs[0], last, PAIR, 0), (d_refs[0], 0, PAIR, 2 * PAIR)):
        upper, lower = slice(row, row + B), slice(row + B, row + 2 * B)
        first_block, second = (
            own_ref[rows, near + at : near + at + B].astype(jnp.float32)
            for rows, at in ((upper, 0), (lower, B))
        )
        i, j = grid()
        out[0:B, :] = jnp.where(j >= i, first_block, second).astype(out.dtype)
        diagonal = jnp.sum(jnp.where(i == j, second, 0.0), axis=0, keepdims=True)
        out[5 * B : HEAD, :] = jnp.broadcast_to(diagonal, (HEAD - 5 * B, B)).astype(out.dtype)
        out[B : 2 * B, :] = own_ref[upper, near + B : near + 2 * B]
        out[2 * B : 3 * B, :] = own_ref[upper, mid : mid + B]
        out[3 * B : 4 * B, :] = (
            own_ref[upper, mid + B : mid + 2 * B] + own_ref[lower, mid : mid + B]
        )
        out[4 * B : 5 * B, :] = own_ref[lower, mid + B : mid + 2 * B]
    for refs, layout, edge in ((x_refs, TO_X, pairs - 1), (d_refs, DIRECT + VIA_X, 0)):
        slab = 0
        for ref, (head, slabs) in zip(refs, layout, strict=True):
            for s in range(slabs):
                at = head + s * PAIR
                ref[at : at + PAIR, :] = v_ref[natural(edge, pairs), slab * B : (slab + 1) * B]
                slab += 1


def scales(scales_ref):
    return scales_ref[0:1, 0:1], scales_ref[1:2, 0:1]


def core_kernel(scales_ref, v_ref, own_ref, one_ref, g0_ref, g2_ref, h0_ref, h1_ref, h2_ref):
    pairs = v_ref.shape[0] // PAIR
    center, halfwidth = scales(scales_ref)
    for at in range(0, v_ref.shape[1], STEP):
        lanes = slice(at, at + STEP)
        v0, v1, v2 = (v_ref[natural(j, pairs), lanes] for j in range(3))
        v = jnp.concatenate([v0, v1, v2], axis=0)
        g0_ref[:, lanes] = dot(own_ref[0:PAIR, PAIR:], v[: 2 * PAIR])
        g2_ref[:, lanes] = dot(own_ref[2 * PAIR :, : 2 * PAIR], v[PAIR:])
        image = dot(own_ref[PAIR : 2 * PAIR, :], v)
        one = ((image - center * v1.astype(jnp.float32)) / halfwidth).astype(one_ref.dtype)
        one_ref[:, lanes] = one
        h0_ref[:, lanes] = dot(own_ref[0:PAIR, 2 * PAIR :], one)
        h1_ref[:, lanes] = dot(own_ref[PAIR : 2 * PAIR, PAIR : 2 * PAIR], one)
        h2_ref[:, lanes] = dot(own_ref[2 * PAIR :, 0:PAIR], one)


def halo_kernel(side, own_ref, sent_ref, halo_ref):
    odd = lax.rem(place(), 2)
    halo_ref[...] = jnp.zeros_like(halo_ref)
    if side == 0:
        known, low = own_ref[0:PAIR, 0:PAIR], odd
    else:
        known, low = own_ref[2 * PAIR :, 2 * PAIR :], 1 - odd
    halo_ref[:, 0:PAIR] = turn(known)
    near, far = PAIR, 2 * PAIR
    halves = sent_ref[0:B, :].astype(jnp.float32)
    i, j = grid()
    diagonal = jnp.broadcast_to(sent_ref[5 * B : HEAD, :].astype(jnp.float32)[0:1], (B, B))
    halo_ref[0:B, near : near + B] = jnp.where(j >= i, halves, halves.T).astype(halo_ref.dtype)
    halo_ref[B:PAIR, near + B : near + PAIR] = jnp.where(
        j < i, halves, jnp.where(j > i, halves.T, diagonal)
    ).astype(halo_ref.dtype)
    halo_ref[0:B, near + B : near + PAIR] = sent_ref[B : 2 * B, :]
    halo_ref[B:PAIR, near : near + B] = turn(sent_ref[B : 2 * B, :])
    halo_ref[0:B, far : far + B] = sent_ref[2 * B : 3 * B, :]
    halo_ref[
        pl.ds(pl.multiple_of(low * B, B), B), pl.ds(pl.multiple_of(far + (1 - low) * B, B), B)
    ] = sent_ref[3 * B : 4 * B, :]
    halo_ref[B:PAIR, far + B : far + PAIR] = sent_ref[4 * B : 5 * B, :]


def far_kernel(side, v_ref, halo_ref, low_ref, high_ref, far_ref):
    pairs = v_ref.shape[0] // PAIR
    band = jnp.concatenate([halo_ref[:, :PAIR], halo_ref[:, 2 * PAIR :]], axis=1)
    for at in range(0, v_ref.shape[1], STEP):
        lanes = slice(at, at + STEP)
        edge = v_ref[natural(0 if side == 0 else 2, pairs), lanes]
        far_ref[:, lanes] = dot(
            band, jnp.concatenate([edge, low_ref[:, lanes], high_ref[:, lanes]], axis=0)
        )


def side_kernel(side, first_slab, held_slab, layout, scales_ref, v_ref, own_ref, halo_ref, far_ref, *refs):
    near_refs, refs = refs[: len(layout)], refs[len(layout) :]
    if side == 0:
        g_ref, h_ref, h1_ref, h1_out, end_out = refs
    else:
        g_ref, h_ref, h1_ref, one_ref, zero_ref = refs[:5]
        out_ref, end_ref, mid_ref, sems = refs[-4:]
    pairs = v_ref.shape[0] // PAIR
    center, halfwidth = scales(scales_ref)
    edge = 0 if side == 0 else 2
    rows = slice(edge * PAIR, (edge + 1) * PAIR)
    outward = slice(0, PAIR) if side == 0 else slice(2 * PAIR, 3 * PAIR)
    slabs = [
        near_ref[head + s * PAIR : head + (s + 1) * PAIR, :]
        for near_ref, (head, count) in zip(near_refs, layout, strict=True)
        for s in range(count)
    ]
    width = len(slabs) * B
    all_lanes = slice(first_slab * B, first_slab * B + width)
    copies = []
    if side == 1:
        copies = [
            pltpu.make_async_copy(source, out_ref.at[natural(pair, pairs), all_lanes], sems.at[pair])
            for pair, source in ((1, mid_ref), (2, end_ref))
        ]
        if held_slab == first_slab:
            held = slice(held_slab * B, held_slab * B + zero_ref.shape[1])
            copies.insert(
                0, pltpu.make_async_copy(zero_ref, out_ref.at[natural(0, pairs), held], sems.at[0])
            )
            copies[0].start()
    for at in range(0, width, STEP):
        to = min(at + STEP, width)
        lanes = slice(first_slab * B + at, first_slab * B + to)
        here = slice(at, to)
        held = slice((first_slab - held_slab) * B + at, (first_slab - held_slab) * B + to)
        near = jnp.concatenate(slabs[at // B : to // B], axis=1)
        v = v_ref[natural(edge, pairs), lanes]
        v32 = v.astype(jnp.float32)
        by_near = dot(jnp.concatenate([own_ref[rows, outward], halo_ref[:, PAIR : 2 * PAIR]], axis=0), near)
        image = g_ref[:, lanes] + by_near[:PAIR]
        edge_one = ((image - center * v32) / halfwidth).astype(v.dtype)
        image = by_near[PAIR:] + far_ref[:, lanes]
        near_one = ((image - center * near.astype(jnp.float32)) / halfwidth).astype(v.dtype)
        by_edge = dot(
            jnp.concatenate([own_ref[PAIR : 2 * PAIR, outward], own_ref[rows, PAIR : 2 * PAIR]], axis=0),
            edge_one,
        )
        h1 = by_edge[:PAIR]
        if side == 0:
            h1_out[:, here] = h1_ref[:, lanes] + h1
        else:
            h1 += h1_ref[:, held]
            one = one_ref[:, lanes].astype(jnp.float32)
            v1 = v_ref[natural(1, pairs), lanes].astype(jnp.float32)
            mid_ref[:, here] = (2.0 * ((h1 - center * one) / halfwidth) - v1).astype(v.dtype)
        image = h_ref[:, lanes] + (by_edge[PAIR:] + dot(own_ref[rows, outward], near_one))
        end = (2.0 * ((image - center * edge_one.astype(jnp.float32)) / halfwidth) - v32).astype(v.dtype)
        if side == 0:
            end_out[:, here] = end
        else:
            end_ref[:, here] = end
    for copy in copies[-2:]:
        copy.start()
    for copy in copies:
        copy.wait()


def whole(ref_space=pltpu.VMEM):
    return pl.BlockSpec(memory_space=ref_space)


def call(body, outs, args, name, aliases=None, scratch=()):
    aliases = aliases or {}

    def in_hbm(out):
        return isinstance(out, jax.ShapeDtypeStruct)

    spaces = [
        pltpu.SMEM
        if a.size < 1024
        else pl.ANY
        if i in aliases and in_hbm(outs[aliases[i]])
        else pltpu.VMEM
        for i, a in enumerate(args)
    ]
    return pl.pallas_call(
        body,
        out_shape=outs,
        in_specs=[whole(space) for space in spaces],
        out_specs=[whole(pl.ANY if in_hbm(out) else pltpu.VMEM) for out in outs],
        scratch_shapes=scratch,
        input_output_aliases=aliases,
        compiler_params=LIMIT,
        cost_estimate=FREE,
        name=name,
    )(
        *(
            pltpu.with_memory_space_constraint(a, pltpu.VMEM) if space == pltpu.VMEM else a
            for a, space in zip(args, spaces, strict=True)
        )
    )


def after(token, value):
    return lax.optimization_barrier((token, value))


def per_device(vectors, ham_blocks, ham_columns, bounds):
    rows, vec_width = vectors.shape
    rows_here = ham_blocks.shape[0]
    ring = lax.axis_size(AXES)
    dtype = vectors.dtype
    over_x = [(i, i ^ 1) for i in range(ring)]
    direct = [(i, (i + 1) % ring if i % 2 else (i - 1) % ring) for i in range(ring)]
    onward = [(i, (i - 2) % ring if i % 2 else (i + 2) % ring) for i in range(ring)]

    def send(part, perm):
        return lax.ppermute(part, AXES, perm)

    low = lax.slice_in_dim(vectors, rows // 2 - B, rows // 2, axis=0)
    low, rest = after(low, vectors)
    middle = [low, lax.slice_in_dim(rest, rows // 2, rows // 2 + B, axis=0)]
    scale, own, *parts = call(
        functools.partial(pack_kernel, ring * rows_here),
        [pltpu.VMEM((8, B), jnp.float32), pltpu.VMEM((rows, 3 * PAIR), dtype)]
        + [
            pltpu.VMEM((head + slabs * PAIR, B), dtype) for head, slabs in TO_X + DIRECT + VIA_X
        ],
        [ham_columns, bounds, ham_blocks, rest],
        "pack",
    )
    to_x, parts = parts[: len(TO_X)], parts[len(TO_X) :]
    to_d, via_x = parts[: len(DIRECT)], parts[len(DIRECT) :]

    far_x = [send(part, over_x) for part in middle]
    near_d = [send(part, direct) for part in to_d]
    far_d = [send(part, onward) for part in far_x]
    passing = [send(part, over_x) for part in via_x]
    far_d[1], passing[1] = after(far_d[1], passing[1])
    near_d += [send(part, onward) for part in passing]
    passing[0], to_x[0] = after(passing[0], to_x[0])
    near_d[0], to_x[0] = after(near_d[0], to_x[0])
    far_d[0], to_x[0] = after(far_d[0], to_x[0])
    passing[1], to_x[1] = after(passing[1], to_x[1])

    wide = lambda kind: pltpu.VMEM((PAIR, vec_width), kind)
    one, g0, g2, h0, h1, h2 = call(
        core_kernel, [wide(dtype)] + [wide(jnp.float32)] * 5, [scale, vectors, own], "core"
    )
    band = [pltpu.VMEM((PAIR, 3 * PAIR), dtype)]
    (halo_d,) = call(functools.partial(halo_kernel, 0), band, [own, near_d[0]], "halo_d")
    far = [wide(jnp.float32)]
    (by_far_d,) = call(functools.partial(far_kernel, 0), far, [vectors, halo_d, *far_d], "far_d")
    result, mid, zero = None, None, None
    first_slab, held_slab, c = 0, 0, -1
    for part, (head, slabs) in zip(to_x, TO_X, strict=True):
        near = None if first_slab else send(part, over_x)
        if mid is None or first_slab * B == held_slab * B + mid.shape[1]:
            c += 1
            held_slab = first_slab
            layout, near_c = ((DIRECT + VIA_X)[:2], near_d[:2]) if c == 0 else (VIA_X[c : c + 1], near_d[c + 1 : c + 2])
            if result is not None:
                near_c[0], result = after(near_c[0], result)
            width = sum(count for _, count in layout) * B
            mid, zero = call(
                functools.partial(side_kernel, 0, first_slab, held_slab, layout),
                [pltpu.VMEM((PAIR, width), jnp.float32), pltpu.VMEM((PAIR, width), dtype)],
                [scale, vectors, own, halo_d, by_far_d, *near_c, g0, h0, h1],
                "side_d",
            )
        if near is None:
            near = send(part, over_x)
        if held_slab == first_slab:
            near, zero = after(near, zero)
        else:
            near, result = after(near, result)
        if result is None:
            (halo_x,) = call(functools.partial(halo_kernel, 1), band, [own, near], "halo_x")
            (by_far_x,) = call(
                functools.partial(far_kernel, 1), far, [vectors, halo_x, *far_x], "far_x"
            )
        args = [scale, vectors, own, halo_x, by_far_x, near, g2, h2, mid, one, zero]
        aliases = {}
        if result is not None:
            aliases[len(args)] = 0
            args.append(result)
        (result,) = call(
            functools.partial(side_kernel, 1, first_slab, held_slab, ((head, slabs),)),
            [jax.ShapeDtypeStruct((rows, vec_width), dtype)],
            args,
            "side_x",
            aliases=aliases,
            scratch=[pltpu.VMEM((PAIR, slabs * B), dtype)] * 2 + [pltpu.SemaphoreType.DMA((3,))],
        )
        first_slab += slabs
    return result


def solution(mesh):
    return jax.shard_map(
        per_device,
        mesh=mesh,
        in_specs=(P(AXES, None), P(AXES, None, None, None), P(AXES, None), P()),
        out_specs=P(AXES, None),
        check_vma=False,
    )
```

```python
import functools

import jax
import jax.numpy as jnp
from jax import lax
from jax.experimental import pallas as pl
from jax.experimental.pallas import tpu as pltpu
from jax.sharding import PartitionSpec as P

AXES = ("row", "col")
B = 128
PAIR = 2 * B
LAST = 4 * B
STEP = 4 * B
HEAD = 5 * B + 16
LIMIT = pltpu.CompilerParams(vmem_limit_bytes=16 * 1024 * 1024)
FREE = pl.CostEstimate(flops=0, bytes_accessed=0, transcendentals=0)
TO_X = ((HEAD, 4), (0, 4), )
DIRECT = ((HEAD, 0),)
VIA_X = ((0, 4), (0, 4))


def place():
    return lax.axis_index("row") * lax.axis_size("col") + lax.axis_index("col")


def dot(a, b):
    return jnp.dot(a, b, preferred_element_type=jnp.float32)


def turn(block):
    return block.astype(jnp.float32).T.astype(block.dtype)


def grid():
    return (lax.broadcasted_iota(jnp.int32, (B, B), axis) for axis in (0, 1))


def natural(pair, pairs):
    odd = lax.rem(place(), 2)
    return pl.ds(pl.multiple_of(jnp.where(odd == 1, pairs - 1 - pair, pair) * PAIR, PAIR), PAIR)


def pack_kernel(total_blocks, cols_ref, bounds_ref, blocks_ref, v_ref, scales_ref, own_ref, *sent):
    low, high = bounds_ref[0], bounds_ref[1]
    scales_ref[0:1, :] = jnp.full((1, B), 0.5 * (high + low), jnp.float32)
    scales_ref[1:2, :] = jnp.full((1, B), 0.5 * (high - low), jnp.float32)
    x_refs, d_refs = sent[: len(TO_X)], sent[len(TO_X) :]
    here = place()
    odd = lax.rem(here, 2)
    rows_here, slots = blocks_ref.shape[0], blocks_ref.shape[1]
    pairs = rows_here // 2
    first = here * rows_here
    own_ref[...] = jnp.zeros_like(own_ref)
    for r in range(rows_here):
        j, i = r // 2, r % 2
        row = pl.multiple_of(jnp.where(odd == 1, pairs - 1 - j, j) * PAIR + i * B, B)
        for k in range(slots):
            offset = lax.rem(cols_ref[r, k] - (first + r) + 2 + total_blocks, total_blocks)
            at = offset + i
            turned = (2 - at // 2) * 2 + lax.rem(at, 2)
            col = pl.multiple_of(jnp.where(odd == 1, turned, at) * B, B)
            own_ref[pl.ds(row, B), pl.ds(col, B)] += blocks_ref[r, k]
    last = (pairs - 1) * PAIR
    for out, row, near, mid in ((x_refs[0], last, PAIR, 0), (d_refs[0], 0, PAIR, 2 * PAIR)):
        upper, lower = slice(row, row + B), slice(row + B, row + 2 * B)
        first_block, second = (
            own_ref[rows, near + at : near + at + B].astype(jnp.float32)
            for rows, at in ((upper, 0), (lower, B))
        )
        i, j = grid()
        out[0:B, :] = jnp.where(j >= i, first_block, second).astype(out.dtype)
        diagonal = jnp.sum(jnp.where(i == j, second, 0.0), axis=0, keepdims=True)
        out[5 * B : HEAD, :] = jnp.broadcast_to(diagonal, (HEAD - 5 * B, B)).astype(out.dtype)
        out[B : 2 * B, :] = own_ref[upper, near + B : near + 2 * B]
        out[2 * B : 3 * B, :] = own_ref[upper, mid : mid + B]
        out[3 * B : 4 * B, :] = (
            own_ref[upper, mid + B : mid + 2 * B] + own_ref[lower, mid : mid + B]
        )
        out[4 * B : 5 * B, :] = own_ref[lower, mid + B : mid + 2 * B]
    for refs, layout, edge in ((x_refs, TO_X, pairs - 1), (d_refs, DIRECT + VIA_X, 0)):
        slab = 0
        for ref, (head, slabs) in zip(refs, layout, strict=True):
            for s in range(slabs):
                at = head + s * PAIR
                ref[at : at + PAIR, :] = v_ref[natural(edge, pairs), slab * B : (slab + 1) * B]
                slab += 1


def scales(scales_ref):
    return scales_ref[0:1, 0:1], scales_ref[1:2, 0:1]


def core_kernel(scales_ref, v_ref, own_ref, one_ref, g0_ref, g2_ref, h0_ref, h1_ref, h2_ref):
    pairs = v_ref.shape[0] // PAIR
    center, halfwidth = scales(scales_ref)
    for at in range(0, v_ref.shape[1], STEP):
        lanes = slice(at, at + STEP)
        v0, v1, v2 = (v_ref[natural(j, pairs), lanes] for j in range(3))
        v = jnp.concatenate([v0, v1, v2], axis=0)
        g0_ref[:, lanes] = dot(own_ref[0:PAIR, PAIR:], v[: 2 * PAIR])
        g2_ref[:, lanes] = dot(own_ref[2 * PAIR :, : 2 * PAIR], v[PAIR:])
        image = dot(own_ref[PAIR : 2 * PAIR, :], v)
        one = ((image - center * v1.astype(jnp.float32)) / halfwidth).astype(one_ref.dtype)
        one_ref[:, lanes] = one
        h0_ref[:, lanes] = dot(own_ref[0:PAIR, 2 * PAIR :], one)
        h1_ref[:, lanes] = dot(own_ref[PAIR : 2 * PAIR, PAIR : 2 * PAIR], one)
        h2_ref[:, lanes] = dot(own_ref[2 * PAIR :, 0:PAIR], one)


def halo_kernel(side, own_ref, sent_ref, halo_ref):
    odd = lax.rem(place(), 2)
    halo_ref[...] = jnp.zeros_like(halo_ref)
    if side == 0:
        known, low = own_ref[0:PAIR, 0:PAIR], odd
    else:
        known, low = own_ref[2 * PAIR :, 2 * PAIR :], 1 - odd
    halo_ref[:, 0:PAIR] = turn(known)
    near, far = PAIR, 2 * PAIR
    halves = sent_ref[0:B, :].astype(jnp.float32)
    i, j = grid()
    diagonal = jnp.broadcast_to(sent_ref[5 * B : HEAD, :].astype(jnp.float32)[0:1], (B, B))
    halo_ref[0:B, near : near + B] = jnp.where(j >= i, halves, halves.T).astype(halo_ref.dtype)
    halo_ref[B:PAIR, near + B : near + PAIR] = jnp.where(
        j < i, halves, jnp.where(j > i, halves.T, diagonal)
    ).astype(halo_ref.dtype)
    halo_ref[0:B, near + B : near + PAIR] = sent_ref[B : 2 * B, :]
    halo_ref[B:PAIR, near : near + B] = turn(sent_ref[B : 2 * B, :])
    halo_ref[0:B, far : far + B] = sent_ref[2 * B : 3 * B, :]
    halo_ref[
        pl.ds(pl.multiple_of(low * B, B), B), pl.ds(pl.multiple_of(far + (1 - low) * B, B), B)
    ] = sent_ref[3 * B : 4 * B, :]
    halo_ref[B:PAIR, far + B : far + PAIR] = sent_ref[4 * B : 5 * B, :]


def far_kernel(side, v_ref, halo_ref, low_ref, high_ref, far_ref):
    pairs = v_ref.shape[0] // PAIR
    band = jnp.concatenate([halo_ref[:, :PAIR], halo_ref[:, 2 * PAIR :]], axis=1)
    for at in range(0, v_ref.shape[1], STEP):
        lanes = slice(at, at + STEP)
        edge = v_ref[natural(0 if side == 0 else 2, pairs), lanes]
        far_ref[:, lanes] = dot(
            band, jnp.concatenate([edge, low_ref[:, lanes], high_ref[:, lanes]], axis=0)
        )


def side_kernel(side, first_slab, held_slab, layout, scales_ref, v_ref, own_ref, halo_ref, far_ref, *refs):
    near_refs, refs = refs[: len(layout)], refs[len(layout) :]
    if side == 0:
        g_ref, h_ref, h1_ref, h1_out, end_out = refs
    else:
        g_ref, h_ref, h1_ref, one_ref, zero_ref = refs[:5]
        out_ref, end_ref, mid_ref, sems = refs[-4:]
    pairs = v_ref.shape[0] // PAIR
    center, halfwidth = scales(scales_ref)
    edge = 0 if side == 0 else 2
    rows = slice(edge * PAIR, (edge + 1) * PAIR)
    outward = slice(0, PAIR) if side == 0 else slice(2 * PAIR, 3 * PAIR)
    slabs = [
        near_ref[head + s * PAIR : head + (s + 1) * PAIR, :]
        for near_ref, (head, count) in zip(near_refs, layout, strict=True)
        for s in range(count)
    ]
    width = len(slabs) * B
    step = STEP if side == 0 else LAST
    copies = []

    def put(pair, source, columns):
        copies.append(
            pltpu.make_async_copy(
                source, out_ref.at[natural(pair, pairs), columns], sems.at[len(copies)]
            )
        )
        copies[-1].start()

    if side == 1 and held_slab == first_slab:
        put(0, zero_ref, slice(held_slab * B, held_slab * B + zero_ref.shape[1]))
    for at in range(0, width, step):
        to = min(at + step, width)
        lanes = slice(first_slab * B + at, first_slab * B + to)
        here = slice(at, to)
        held = slice((first_slab - held_slab) * B + at, (first_slab - held_slab) * B + to)
        near = jnp.concatenate(slabs[at // B : to // B], axis=1)
        v = v_ref[natural(edge, pairs), lanes]
        v32 = v.astype(jnp.float32)
        by_near = dot(jnp.concatenate([own_ref[rows, outward], halo_ref[:, PAIR : 2 * PAIR]], axis=0), near)
        image = g_ref[:, lanes] + by_near[:PAIR]
        edge_one = ((image - center * v32) / halfwidth).astype(v.dtype)
        image = by_near[PAIR:] + far_ref[:, lanes]
        near_one = ((image - center * near.astype(jnp.float32)) / halfwidth).astype(v.dtype)
        by_edge = dot(
            jnp.concatenate([own_ref[PAIR : 2 * PAIR, outward], own_ref[rows, PAIR : 2 * PAIR]], axis=0),
            edge_one,
        )
        h1 = by_edge[:PAIR]
        if side == 0:
            h1_out[:, here] = h1_ref[:, lanes] + h1
        else:
            h1 += h1_ref[:, held]
            one = one_ref[:, lanes].astype(jnp.float32)
            v1 = v_ref[natural(1, pairs), lanes].astype(jnp.float32)
            mid_ref[:, here] = (2.0 * ((h1 - center * one) / halfwidth) - v1).astype(v.dtype)
            put(1, mid_ref.at[:, here], lanes)
        image = h_ref[:, lanes] + (by_edge[PAIR:] + dot(own_ref[rows, outward], near_one))
        end = (2.0 * ((image - center * edge_one.astype(jnp.float32)) / halfwidth) - v32).astype(v.dtype)
        if side == 0:
            end_out[:, here] = end
        else:
            end_ref[:, here] = end
            put(2, end_ref.at[:, here], lanes)
    for copy in copies:
        copy.wait()


def whole(ref_space=pltpu.VMEM):
    return pl.BlockSpec(memory_space=ref_space)


def call(body, outs, args, name, aliases=None, scratch=()):
    aliases = aliases or {}

    def in_hbm(out):
        return isinstance(out, jax.ShapeDtypeStruct)

    spaces = [
        pltpu.SMEM
        if a.size < 1024
        else pl.ANY
        if i in aliases and in_hbm(outs[aliases[i]])
        else pltpu.VMEM
        for i, a in enumerate(args)
    ]
    return pl.pallas_call(
        body,
        out_shape=outs,
        in_specs=[whole(space) for space in spaces],
        out_specs=[whole(pl.ANY if in_hbm(out) else pltpu.VMEM) for out in outs],
        scratch_shapes=scratch,
        input_output_aliases=aliases,
        compiler_params=LIMIT,
        cost_estimate=FREE,
        name=name,
    )(
        *(
            pltpu.with_memory_space_constraint(a, pltpu.VMEM) if space == pltpu.VMEM else a
            for a, space in zip(args, spaces, strict=True)
        )
    )


def after(token, value):
    return lax.optimization_barrier((token, value))


def per_device(vectors, ham_blocks, ham_columns, bounds):
    rows, vec_width = vectors.shape
    rows_here = ham_blocks.shape[0]
    ring = lax.axis_size(AXES)
    dtype = vectors.dtype
    over_x = [(i, i ^ 1) for i in range(ring)]
    direct = [(i, (i + 1) % ring if i % 2 else (i - 1) % ring) for i in range(ring)]
    onward = [(i, (i - 2) % ring if i % 2 else (i + 2) % ring) for i in range(ring)]

    def send(part, perm):
        return lax.ppermute(part, AXES, perm)

    low = lax.slice_in_dim(vectors, rows // 2 - B, rows // 2, axis=0)
    low, rest = after(low, vectors)
    middle = [low, lax.slice_in_dim(rest, rows // 2, rows // 2 + B, axis=0)]
    scale, own, *parts = call(
        functools.partial(pack_kernel, ring * rows_here),
        [pltpu.VMEM((8, B), jnp.float32), pltpu.VMEM((rows, 3 * PAIR), dtype)]
        + [
            pltpu.VMEM((head + slabs * PAIR, B), dtype) for head, slabs in TO_X + DIRECT + VIA_X
        ],
        [ham_columns, bounds, ham_blocks, rest],
        "pack",
    )
    to_x, parts = parts[: len(TO_X)], parts[len(TO_X) :]
    to_d, via_x = parts[: len(DIRECT)], parts[len(DIRECT) :]

    far_x = [send(part, over_x) for part in middle]
    near_d = [send(part, direct) for part in to_d]
    far_d = [send(part, onward) for part in far_x]
    passing = [send(part, over_x) for part in via_x]
    far_d[1], passing[1] = after(far_d[1], passing[1])
    near_d += [send(part, onward) for part in passing]
    passing[0], to_x[0] = after(passing[0], to_x[0])
    near_d[0], to_x[0] = after(near_d[0], to_x[0])
    far_d[0], to_x[0] = after(far_d[0], to_x[0])
    passing[1], to_x[1] = after(passing[1], to_x[1])

    wide = lambda kind: pltpu.VMEM((PAIR, vec_width), kind)
    one, g0, g2, h0, h1, h2 = call(
        core_kernel, [wide(dtype)] + [wide(jnp.float32)] * 5, [scale, vectors, own], "core"
    )
    band = [pltpu.VMEM((PAIR, 3 * PAIR), dtype)]
    (halo_d,) = call(functools.partial(halo_kernel, 0), band, [own, near_d[0]], "halo_d")
    far = [wide(jnp.float32)]
    (by_far_d,) = call(functools.partial(far_kernel, 0), far, [vectors, halo_d, *far_d], "far_d")
    result, mid, zero = None, None, None
    first_slab, held_slab, c = 0, 0, -1
    for part, (head, slabs) in zip(to_x, TO_X, strict=True):
        near = None if first_slab else send(part, over_x)
        if mid is None or first_slab * B == held_slab * B + mid.shape[1]:
            c += 1
            held_slab = first_slab
            layout, near_c = ((DIRECT + VIA_X)[:2], near_d[:2]) if c == 0 else (VIA_X[c : c + 1], near_d[c + 1 : c + 2])
            if result is not None:
                near_c[0], result = after(near_c[0], result)
            width = sum(count for _, count in layout) * B
            mid, zero = call(
                functools.partial(side_kernel, 0, first_slab, held_slab, layout),
                [pltpu.VMEM((PAIR, width), jnp.float32), pltpu.VMEM((PAIR, width), dtype)],
                [scale, vectors, own, halo_d, by_far_d, *near_c, g0, h0, h1],
                "side_d",
            )
        if near is None:
            near = send(part, over_x)
        if held_slab == first_slab:
            near, zero = after(near, zero)
        else:
            near, result = after(near, result)
        if result is None:
            (halo_x,) = call(functools.partial(halo_kernel, 1), band, [own, near], "halo_x")
            (by_far_x,) = call(
                functools.partial(far_kernel, 1), far, [vectors, halo_x, *far_x], "far_x"
            )
        args = [scale, vectors, own, halo_x, by_far_x, near, g2, h2, mid, one, zero]
        aliases = {}
        if result is not None:
            aliases[len(args)] = 0
            args.append(result)
        (result,) = call(
            functools.partial(side_kernel, 1, first_slab, held_slab, ((head, slabs),)),
            [jax.ShapeDtypeStruct((rows, vec_width), dtype)],
            args,
            "side_x",
            aliases=aliases,
            scratch=[pltpu.VMEM((PAIR, slabs * B), dtype)] * 2 + [
                pltpu.SemaphoreType.DMA((1 + 2 * pl.cdiv(slabs * B, LAST),))
            ],
        )
        first_slab += slabs
    return result


def solution(mesh):
    return jax.shard_map(
        per_device,
        mesh=mesh,
        in_specs=(P(AXES, None), P(AXES, None, None, None), P(AXES, None), P()),
        out_specs=P(AXES, None),
        check_vma=False,
    )
```

```python
import functools

import jax
import jax.numpy as jnp
from jax import lax
from jax.experimental import pallas as pl
from jax.experimental.pallas import tpu as pltpu
from jax.sharding import PartitionSpec as P

AXES = ("row", "col")
B = 128
PAIR = 2 * B
STEP = 4 * B
HEAD = 5 * B + 16
LIMIT = pltpu.CompilerParams(vmem_limit_bytes=16 * 1024 * 1024)
FREE = pl.CostEstimate(flops=0, bytes_accessed=0, transcendentals=0)
TO_X = ((HEAD, 4), (0, 4), )
DIRECT = ((HEAD, 0),)
VIA_X = ((0, 4), (0, 4))


def place():
    return lax.axis_index("row") * lax.axis_size("col") + lax.axis_index("col")


def dot(a, b):
    return jnp.dot(a, b, preferred_element_type=jnp.float32)


def turn(block):
    return block.astype(jnp.float32).T.astype(block.dtype)


def grid():
    return (lax.broadcasted_iota(jnp.int32, (B, B), axis) for axis in (0, 1))


def natural(pair, pairs):
    odd = lax.rem(place(), 2)
    return pl.ds(pl.multiple_of(jnp.where(odd == 1, pairs - 1 - pair, pair) * PAIR, PAIR), PAIR)


def pack_kernel(total_blocks, cols_ref, bounds_ref, blocks_ref, v_ref, scales_ref, own_ref, *sent):
    low, high = bounds_ref[0], bounds_ref[1]
    scales_ref[0:1, :] = jnp.full((1, B), 0.5 * (high + low), jnp.float32)
    scales_ref[1:2, :] = jnp.full((1, B), 0.5 * (high - low), jnp.float32)
    x_refs, d_refs = sent[: len(TO_X)], sent[len(TO_X) :]
    here = place()
    odd = lax.rem(here, 2)
    rows_here, slots = blocks_ref.shape[0], blocks_ref.shape[1]
    pairs = rows_here // 2
    first = here * rows_here
    own_ref[...] = jnp.zeros_like(own_ref)
    for r in range(rows_here):
        j, i = r // 2, r % 2
        row = pl.multiple_of(jnp.where(odd == 1, pairs - 1 - j, j) * PAIR + i * B, B)
        for k in range(slots):
            offset = lax.rem(cols_ref[r, k] - (first + r) + 2 + total_blocks, total_blocks)
            at = offset + i
            turned = (2 - at // 2) * 2 + lax.rem(at, 2)
            col = pl.multiple_of(jnp.where(odd == 1, turned, at) * B, B)
            own_ref[pl.ds(row, B), pl.ds(col, B)] += blocks_ref[r, k]
    last = (pairs - 1) * PAIR
    for out, row, near, mid in ((x_refs[0], last, PAIR, 0), (d_refs[0], 0, PAIR, 2 * PAIR)):
        upper, lower = slice(row, row + B), slice(row + B, row + 2 * B)
        first_block, second = (
            own_ref[rows, near + at : near + at + B].astype(jnp.float32)
            for rows, at in ((upper, 0), (lower, B))
        )
        i, j = grid()
        out[0:B, :] = jnp.where(j >= i, first_block, second).astype(out.dtype)
        diagonal = jnp.sum(jnp.where(i == j, second, 0.0), axis=0, keepdims=True)
        out[5 * B : HEAD, :] = jnp.broadcast_to(diagonal, (HEAD - 5 * B, B)).astype(out.dtype)
        out[B : 2 * B, :] = own_ref[upper, near + B : near + 2 * B]
        out[2 * B : 3 * B, :] = own_ref[upper, mid : mid + B]
        out[3 * B : 4 * B, :] = (
            own_ref[upper, mid + B : mid + 2 * B] + own_ref[lower, mid : mid + B]
        )
        out[4 * B : 5 * B, :] = own_ref[lower, mid + B : mid + 2 * B]
    for refs, layout, edge in ((x_refs, TO_X, pairs - 1), (d_refs, DIRECT + VIA_X, 0)):
        slab = 0
        for ref, (head, slabs) in zip(refs, layout, strict=True):
            for s in range(slabs):
                at = head + s * PAIR
                ref[at : at + PAIR, :] = v_ref[natural(edge, pairs), slab * B : (slab + 1) * B]
                slab += 1


def scales(scales_ref):
    return scales_ref[0:1, 0:1], scales_ref[1:2, 0:1]


def core_kernel(scales_ref, v_ref, own_ref, one_ref, g0_ref, g2_ref, h0_ref, h1_ref, h2_ref):
    pairs = v_ref.shape[0] // PAIR
    center, halfwidth = scales(scales_ref)
    for at in range(0, v_ref.shape[1], STEP):
        lanes = slice(at, at + STEP)
        v0, v1, v2 = (v_ref[natural(j, pairs), lanes] for j in range(3))
        v = jnp.concatenate([v0, v1, v2], axis=0)
        g0_ref[:, lanes] = dot(own_ref[0:PAIR, PAIR:], v[: 2 * PAIR])
        g2_ref[:, lanes] = dot(own_ref[2 * PAIR :, : 2 * PAIR], v[PAIR:])
        image = dot(own_ref[PAIR : 2 * PAIR, :], v)
        one = ((image - center * v1.astype(jnp.float32)) / halfwidth).astype(one_ref.dtype)
        one_ref[:, lanes] = one
        h0_ref[:, lanes] = dot(own_ref[0:PAIR, 2 * PAIR :], one)
        h1_ref[:, lanes] = dot(own_ref[PAIR : 2 * PAIR, PAIR : 2 * PAIR], one)
        h2_ref[:, lanes] = dot(own_ref[2 * PAIR :, 0:PAIR], one)


def halo_kernel(side, own_ref, sent_ref, halo_ref):
    odd = lax.rem(place(), 2)
    halo_ref[...] = jnp.zeros_like(halo_ref)
    if side == 0:
        known, low = own_ref[0:PAIR, 0:PAIR], odd
    else:
        known, low = own_ref[2 * PAIR :, 2 * PAIR :], 1 - odd
    halo_ref[:, 0:PAIR] = turn(known)
    near, far = PAIR, 2 * PAIR
    halves = sent_ref[0:B, :].astype(jnp.float32)
    i, j = grid()
    diagonal = jnp.broadcast_to(sent_ref[5 * B : HEAD, :].astype(jnp.float32)[0:1], (B, B))
    halo_ref[0:B, near : near + B] = jnp.where(j >= i, halves, halves.T).astype(halo_ref.dtype)
    halo_ref[B:PAIR, near + B : near + PAIR] = jnp.where(
        j < i, halves, jnp.where(j > i, halves.T, diagonal)
    ).astype(halo_ref.dtype)
    halo_ref[0:B, near + B : near + PAIR] = sent_ref[B : 2 * B, :]
    halo_ref[B:PAIR, near : near + B] = turn(sent_ref[B : 2 * B, :])
    halo_ref[0:B, far : far + B] = sent_ref[2 * B : 3 * B, :]
    halo_ref[
        pl.ds(pl.multiple_of(low * B, B), B), pl.ds(pl.multiple_of(far + (1 - low) * B, B), B)
    ] = sent_ref[3 * B : 4 * B, :]
    halo_ref[B:PAIR, far + B : far + PAIR] = sent_ref[4 * B : 5 * B, :]


def far_kernel(side, v_ref, halo_ref, low_ref, high_ref, far_ref):
    pairs = v_ref.shape[0] // PAIR
    band = jnp.concatenate([halo_ref[:, :PAIR], halo_ref[:, 2 * PAIR :]], axis=1)
    for at in range(0, v_ref.shape[1], STEP):
        lanes = slice(at, at + STEP)
        edge = v_ref[natural(0 if side == 0 else 2, pairs), lanes]
        far_ref[:, lanes] = dot(
            band, jnp.concatenate([edge, low_ref[:, lanes], high_ref[:, lanes]], axis=0)
        )


def side_kernel(side, first_slab, held_slab, layout, scales_ref, v_ref, own_ref, halo_ref, far_ref, *refs):
    near_refs, refs = refs[: len(layout)], refs[len(layout) :]
    if side == 0:
        g_ref, h_ref, h1_ref, h1_out, end_out = refs
    else:
        g_ref, h_ref, h1_ref, one_ref, zero_ref = refs[:5]
        out_ref, end_ref, mid_ref, sems = refs[-4:]
    pairs = v_ref.shape[0] // PAIR
    center, halfwidth = scales(scales_ref)
    edge = 0 if side == 0 else 2
    rows = slice(edge * PAIR, (edge + 1) * PAIR)
    outward = slice(0, PAIR) if side == 0 else slice(2 * PAIR, 3 * PAIR)
    slabs = [
        near_ref[head + s * PAIR : head + (s + 1) * PAIR, :]
        for near_ref, (head, count) in zip(near_refs, layout, strict=True)
        for s in range(count)
    ]
    width = len(slabs) * B
    all_lanes = slice(first_slab * B, first_slab * B + width)
    copies = []
    if side == 1:
        copies = [
            pltpu.make_async_copy(source, out_ref.at[natural(pair, pairs), all_lanes], sems.at[pair])
            for pair, source in ((1, mid_ref), (2, end_ref))
        ]
        if held_slab == first_slab:
            held = slice(held_slab * B, held_slab * B + zero_ref.shape[1])
            copies.insert(
                0, pltpu.make_async_copy(zero_ref, out_ref.at[natural(0, pairs), held], sems.at[0])
            )
            copies[0].start()
    for at in range(0, width, STEP):
        to = min(at + STEP, width)
        lanes = slice(first_slab * B + at, first_slab * B + to)
        here = slice(at, to)
        held = slice((first_slab - held_slab) * B + at, (first_slab - held_slab) * B + to)
        near = jnp.concatenate(slabs[at // B : to // B], axis=1)
        v = v_ref[natural(edge, pairs), lanes]
        v32 = v.astype(jnp.float32)
        by_near = dot(jnp.concatenate([own_ref[rows, outward], halo_ref[:, PAIR : 2 * PAIR]], axis=0), near)
        image = g_ref[:, lanes] + by_near[:PAIR]
        edge_one = ((image - center * v32) / halfwidth).astype(v.dtype)
        image = by_near[PAIR:] + far_ref[:, lanes]
        near_one = ((image - center * near.astype(jnp.float32)) / halfwidth).astype(v.dtype)
        by_edge = dot(
            jnp.concatenate([own_ref[PAIR : 2 * PAIR, outward], own_ref[rows, PAIR : 2 * PAIR]], axis=0),
            edge_one,
        )
        h1 = by_edge[:PAIR]
        if side == 0:
            h1_out[:, here] = h1_ref[:, lanes] + h1
        else:
            h1 += h1_ref[:, held]
            one = one_ref[:, lanes].astype(jnp.float32)
            v1 = v_ref[natural(1, pairs), lanes].astype(jnp.float32)
            mid_ref[:, here] = (2.0 * ((h1 - center * one) / halfwidth) - v1).astype(v.dtype)
        image = h_ref[:, lanes] + (by_edge[PAIR:] + dot(own_ref[rows, outward], near_one))
        end = (2.0 * ((image - center * edge_one.astype(jnp.float32)) / halfwidth) - v32).astype(v.dtype)
        if side == 0:
            end_out[:, here] = end
        else:
            end_ref[:, here] = end
    for copy in copies[-2:]:
        copy.start()
    for copy in copies:
        copy.wait()


def whole(ref_space=pltpu.VMEM):
    return pl.BlockSpec(memory_space=ref_space)


def call(body, outs, args, name, aliases=None, scratch=()):
    aliases = aliases or {}

    def in_hbm(out):
        return isinstance(out, jax.ShapeDtypeStruct)

    spaces = [
        pltpu.SMEM
        if a.size < 1024
        else pl.ANY
        if i in aliases and in_hbm(outs[aliases[i]])
        else pltpu.VMEM
        for i, a in enumerate(args)
    ]
    return pl.pallas_call(
        body,
        out_shape=outs,
        in_specs=[whole(space) for space in spaces],
        out_specs=[whole(pl.ANY if in_hbm(out) else pltpu.VMEM) for out in outs],
        scratch_shapes=scratch,
        input_output_aliases=aliases,
        compiler_params=LIMIT,
        cost_estimate=FREE,
        name=name,
    )(
        *(
            pltpu.with_memory_space_constraint(a, pltpu.VMEM) if space == pltpu.VMEM else a
            for a, space in zip(args, spaces, strict=True)
        )
    )


def after(token, value):
    return lax.optimization_barrier((token, value))


def per_device(vectors, ham_blocks, ham_columns, bounds):
    rows, vec_width = vectors.shape
    rows_here = ham_blocks.shape[0]
    ring = lax.axis_size(AXES)
    dtype = vectors.dtype
    over_x = [(i, i ^ 1) for i in range(ring)]
    direct = [(i, (i + 1) % ring if i % 2 else (i - 1) % ring) for i in range(ring)]
    onward = [(i, (i - 2) % ring if i % 2 else (i + 2) % ring) for i in range(ring)]

    def send(part, perm):
        return lax.ppermute(part, AXES, perm)

    low = lax.slice_in_dim(vectors, rows // 2 - B, rows // 2, axis=0)
    low, rest = after(low, vectors)
    middle = [low, lax.slice_in_dim(rest, rows // 2, rows // 2 + B, axis=0)]
    scale, own, *parts = call(
        functools.partial(pack_kernel, ring * rows_here),
        [pltpu.VMEM((8, B), jnp.float32), pltpu.VMEM((rows, 3 * PAIR), dtype)]
        + [
            pltpu.VMEM((head + slabs * PAIR, B), dtype) for head, slabs in TO_X + DIRECT + VIA_X
        ],
        [ham_columns, bounds, ham_blocks, rest],
        "pack",
    )
    to_x, parts = parts[: len(TO_X)], parts[len(TO_X) :]
    to_d, via_x = parts[: len(DIRECT)], parts[len(DIRECT) :]

    far_x = [send(part, over_x) for part in middle]
    near_d = [send(part, direct) for part in to_d]
    far_x[0], via_x[1] = after(far_x[0], via_x[1])
    far_d = [send(part, onward) for part in far_x]
    passing = [send(part, over_x) for part in via_x]
    far_d[1], passing[1] = after(far_d[1], passing[1])
    near_d += [send(part, onward) for part in passing]
    passing[0], to_x[0] = after(passing[0], to_x[0])
    near_d[0], to_x[0] = after(near_d[0], to_x[0])
    far_d[0], to_x[0] = after(far_d[0], to_x[0])
    passing[1], to_x[1] = after(passing[1], to_x[1])

    wide = lambda kind: pltpu.VMEM((PAIR, vec_width), kind)
    one, g0, g2, h0, h1, h2 = call(
        core_kernel, [wide(dtype)] + [wide(jnp.float32)] * 5, [scale, vectors, own], "core"
    )
    band = [pltpu.VMEM((PAIR, 3 * PAIR), dtype)]
    (halo_d,) = call(functools.partial(halo_kernel, 0), band, [own, near_d[0]], "halo_d")
    far = [wide(jnp.float32)]
    (by_far_d,) = call(functools.partial(far_kernel, 0), far, [vectors, halo_d, *far_d], "far_d")
    result, mid, zero = None, None, None
    first_slab, held_slab, c = 0, 0, -1
    for part, (head, slabs) in zip(to_x, TO_X, strict=True):
        near = None if first_slab else send(part, over_x)
        if mid is None or first_slab * B == held_slab * B + mid.shape[1]:
            c += 1
            held_slab = first_slab
            layout, near_c = ((DIRECT + VIA_X)[:2], near_d[:2]) if c == 0 else (VIA_X[c : c + 1], near_d[c + 1 : c + 2])
            if result is not None:
                near_c[0], result = after(near_c[0], result)
            width = sum(count for _, count in layout) * B
            mid, zero = call(
                functools.partial(side_kernel, 0, first_slab, held_slab, layout),
                [pltpu.VMEM((PAIR, width), jnp.float32), pltpu.VMEM((PAIR, width), dtype)],
                [scale, vectors, own, halo_d, by_far_d, *near_c, g0, h0, h1],
                "side_d",
            )
        if near is None:
            near = send(part, over_x)
        if held_slab == first_slab:
            near, zero = after(near, zero)
        else:
            near, result = after(near, result)
        if result is None:
            (halo_x,) = call(functools.partial(halo_kernel, 1), band, [own, near], "halo_x")
            (by_far_x,) = call(
                functools.partial(far_kernel, 1), far, [vectors, halo_x, *far_x], "far_x"
            )
        args = [scale, vectors, own, halo_x, by_far_x, near, g2, h2, mid, one, zero]
        aliases = {}
        if result is not None:
            aliases[len(args)] = 0
            args.append(result)
        (result,) = call(
            functools.partial(side_kernel, 1, first_slab, held_slab, ((head, slabs),)),
            [jax.ShapeDtypeStruct((rows, vec_width), dtype)],
            args,
            "side_x",
            aliases=aliases,
            scratch=[pltpu.VMEM((PAIR, slabs * B), dtype)] * 2 + [pltpu.SemaphoreType.DMA((3,))],
        )
        first_slab += slabs
    return result


def solution(mesh):
    return jax.shard_map(
        per_device,
        mesh=mesh,
        in_specs=(P(AXES, None), P(AXES, None, None, None), P(AXES, None), P()),
        out_specs=P(AXES, None),
        check_vma=False,
    )
```
